32 devices in a mesh: fsdp: 4 (over z), seq: 8 (over y, x, core).
Axes of the slice: x: 2, y: 2, z: 4, core: 2. Of those that a mesh axis runs over, the one named last changes fastest.
Arguments:
- block_input: bfloat16 [4, 2048, 2048], P('fsdp', 'seq'), may hold values from -6 to 6
- ln_gain: bfloat16 [2048], P(('fsdp', 'seq')), may hold values from 0.5 to 1.5
- norm_layer_bias: bfloat16 [2048], P(('fsdp', 'seq')), may hold values from -1.796875 to 1.796875
- query_key_value_weight: bfloat16 [2048, 6144], P(('fsdp', 'seq')), may hold values from -0.125 to 0.125
- query_key_value_bias: bfloat16 [6144], P(('fsdp', 'seq')), may hold values from -0.29882812 to 0.29882812
- attention_output_weight: bfloat16 [2048, 2048], P(('fsdp', 'seq')), may hold values from -1.5 to 1.5
- attention_output_bias: bfloat16 [2048], P(('fsdp', 'seq')), may hold values from -1.796875 to 1.796875
- first_feed_weight: bfloat16 [2048, 8192], P(('fsdp', 'seq')), may hold values from -0.125 to 0.125
- first_feed_bias: bfloat16 [8192], P(('fsdp', 'seq')), may hold values from -3 to 3
- second_feed_weight: bfloat16 [8192, 2048], P(('fsdp', 'seq')), may hold values from -0.0625 to 0.0625
- second_feed_bias: bfloat16 [2048], P(('fsdp', 'seq')), may hold values from -1.796875 to 1.796875
- cotangent: bfloat16 [4, 2048, 2048], P('fsdp', 'seq'), may hold values from -6 to 6
Outputs:
- block_output: bfloat16 [4, 2048, 2048], P('fsdp', 'seq')
- grad_input: float32 [4, 2048, 2048], P('fsdp', 'seq')
- norm_gain_gradient: float32 [2048], P(('fsdp', 'seq'))
- grad_ln_bias: float32 [2048], P(('fsdp', 'seq'))
- grad_w_qkv: float32 [2048, 6144], P(('fsdp', 'seq'))
- grad_b_qk: float32 [4096], P(('fsdp', 'seq'))
- grad_b_v: float32 [2048], P(('fsdp', 'seq'))
- grad_w_out: float32 [2048, 2048], P(('fsdp', 'seq'))
- grad_b_out: float32 [2048], P(('fsdp', 'seq'))
- grad_w_fc1: float32 [2048, 8192], P(('fsdp', 'seq'))
- grad_b_fc1: float32 [8192], P(('fsdp', 'seq'))
- grad_w_fc2: float32 [8192, 2048], P(('fsdp', 'seq'))
- grad_b_fc2: float32 [2048], P(('fsdp', 'seq'))
The draws below stay inside these ranges and needn't reach their ends.
All inputs are finite; a program needn't handle non-finite values.
Results may differ from the reference program's by a relative error of at most 0.011.
Values may be sent and summed in bfloat16 or wider, within the bound.
No kernel may reach another device: no remote copies, remote signals or barrier semaphores. Data moves between devices by JAX's collectives and lax.ppermute only.
A program may use at most 448 MiB of HBM per device.

```python
import jax
import jax.numpy as jnp
from jax import lax

D = 2048
H = 32
HD = 64
ROT = 32
FF = 8192
LEN = 2048
SEQS = 4


def level_of(key, dims, pieces, low, largest):
    loudness, own = 1.0, jax.random.fold_in(key, 6)
    for axis_at, shards_of in pieces:
        steps = jnp.exp(jax.random.uniform(jax.random.fold_in(own, axis_at), (shards_of,), jnp.float32, low / len(pieces), largest / len(pieces)))
        loudness = loudness * jnp.repeat(steps, dims[axis_at] // shards_of).reshape([-1 if axis == axis_at else 1 for axis in range(len(dims))])
    return loudness


def bell_draw(rng, shape, scale, bound, shards=(), kind=jnp.bfloat16):
    level = level_of(rng, shape, shards, -0.22, 0.18) if shards else 1.0
    values = jax.random.normal(rng, shape, jnp.float32) * scale * level
    return jnp.minimum(jnp.maximum(values, -bound), bound).astype(kind)


def setup_inputs(seed: int = 0) -> dict:
    key_of = jax.random.split(jax.random.key(seed), 13)
    block_input = bell_draw(key_of[0], (SEQS, LEN, D), 1.0, 6.0, ((0, 4), (1, 8)))
    ln_gain = jnp.clip(1.0 + 0.1 * jax.random.normal(key_of[1], (D,), jnp.float32), 0.5, 1.5).astype(jnp.bfloat16)
    norm_layer_bias = bell_draw(key_of[2], (D,), 0.3, 1.796875, ((0, 32),))
    query_key_value_weight = bell_draw(key_of[3], (D, 3 * D), D ** -0.5, 0.125, ((0, 32),))
    query_key_value_bias = bell_draw(key_of[4], (3 * D,), 0.05, 0.29882812, ((0, 32),))
    attention_output_weight = bell_draw(key_of[5], (D, D), (max(1, D // 128)) ** -0.5, 1.5, ((0, 32),))
    attention_output_bias = bell_draw(key_of[6], (D,), 0.3, 1.796875, ((0, 32),))
    first_feed_weight = bell_draw(key_of[7], (D, FF), D ** -0.5, 0.125, ((0, 32),))
    first_feed_bias = bell_draw(key_of[8], (FF,), 0.5, 3.0, ((0, 32),))
    second_feed_weight = bell_draw(key_of[9], (FF, D), FF ** -0.5, 0.0625, ((0, 32),))
    second_feed_bias = bell_draw(key_of[10], (D,), 0.3, 1.796875, ((0, 32),))
    cotangent = bell_draw(key_of[11], (SEQS, LEN, D), 1.0, 6.0, ((0, 4), (1, 8)))
    return {"block_input": block_input, "ln_gain": ln_gain, "norm_layer_bias": norm_layer_bias, "query_key_value_weight": query_key_value_weight, "query_key_value_bias": query_key_value_bias, "attention_output_weight": attention_output_weight, "attention_output_bias": attention_output_bias, "first_feed_weight": first_feed_weight, "first_feed_bias": first_feed_bias, "second_feed_weight": second_feed_weight, "second_feed_bias": second_feed_bias, "cotangent": cotangent}


@jax.custom_vjp
def low(v):
    return lax.optimization_barrier(v.astype(jnp.bfloat16)).astype(jnp.float32)

@jax.custom_vjp
def low_back(v):
    return v

def low_keep(v):
    return (low(v), None)

def low_pass(kept, grad):
    return (grad,)

def back_keep(v):
    return (v, None)

def back_low(kept, grad):
    return (low(grad),)
low.defvjp(low_keep, low_pass)
low_back.defvjp(back_keep, back_low)
EPSILON = 1e-05
HIGH_ACCURACY = lax.Precision.HIGHEST

def layer_norm(values, gain, shift):
    average = lax.optimization_barrier(jnp.mean(values, -1, keepdims=True))
    centred = values - average
    variance = lax.optimization_barrier(jnp.mean(centred * centred, -1, keepdims=True))
    return centred * lax.rsqrt(variance + EPSILON) * gain + shift

def gelu_tanh(values):
    return 0.5 * values * (1.0 + jnp.tanh(0.7978845608028654 * (values + 0.044715 * values * values * values)))

def rotate_heads(projected_rows, positions):
    half_rot = ROT // 2
    freqs = 10000.0 ** (-2.0 * jnp.arange(half_rot).astype(jnp.float32) / ROT)
    angles = positions.astype(jnp.float32)[:, None] * freqs[None, :]
    cosine = jnp.cos(angles)[:, None, :]
    sine = jnp.sin(angles)[:, None, :]
    turned = []
    for which in range(2):
        part = projected_rows[..., which, :, :]
        first = part[..., :half_rot]
        second = part[..., half_rot:ROT]
        turned.append(jnp.concatenate([first * cosine - second * sine, second * cosine + first * sine, part[..., ROT:]], -1))
    turned.append(projected_rows[..., 2, :, :])
    return jnp.stack(turned, -3)

def attend_heads_fn(queries, keys, values):
    length = keys.shape[0]
    block = min(512, length)
    scale = HD ** (-0.5)
    key_pos = jnp.arange(length).astype(jnp.int32)

    def one_block(index):
        start = (index * block).astype(jnp.int32)
        rows = lax.dynamic_slice_in_dim(queries, start, block, 0)
        unprocessed_input = jnp.einsum('qhd,khd->hqk', rows, keys, precision=HIGH_ACCURACY)
        score_matrix = low_back(unprocessed_input * scale)
        query_pos = start + jnp.arange(block).astype(jnp.int32)
        allowed = query_pos[:, None] >= key_pos[None, :]
        score_matrix = jnp.where(allowed[None], score_matrix, -1e+30)
        row_max = lax.optimization_barrier(jnp.max(score_matrix, -1, keepdims=True))
        expo = jnp.exp(score_matrix - row_max)
        probs = expo / lax.optimization_barrier(jnp.sum(expo, -1, keepdims=True))
        return jnp.einsum('hqk,khd->qhd', low(probs), values, precision=HIGH_ACCURACY)
    outs = lax.map(jax.checkpoint(one_block), jnp.arange(length // block).astype(jnp.int32))
    return outs.reshape(length, -1)

def forward(block_in, gain, shift, query_key_value_weight, query_key_value_bias, attention_output_weight, attention_output_bias, first_feed_weight, first_feed_bias, second_feed_weight, second_feed_bias):
    seqs, length, model_width = block_in.shape
    normalized_reduced = low(layer_norm(block_in, gain, shift))
    unprocessed_input = jnp.einsum('iqm,mk->iqk', normalized_reduced, query_key_value_weight, precision=HIGH_ACCURACY) + query_key_value_bias
    projected_rows = low_back(unprocessed_input).reshape(seqs, length, 3, H, HD)
    rotated = low_back(low(rotate_heads(projected_rows, jnp.arange(length).astype(jnp.int32))))

    def per_sequence(item):
        return attend_heads_fn(item[:, 0], item[:, 1], item[:, 2])
    attention_result = low_back(low(lax.map(per_sequence, rotated)))
    up_preactivation = low_back(jnp.einsum('vrm,mk->vrk', normalized_reduced, first_feed_weight, precision=HIGH_ACCURACY) + first_feed_bias)
    up_activation = low(gelu_tanh(up_preactivation))
    attention_portion = jnp.einsum('iqm,mk->iqk', attention_result, attention_output_weight, precision=HIGH_ACCURACY) + attention_output_bias
    feed_forward_portion = jnp.einsum('avi,ie->ave', up_activation, second_feed_weight, precision=HIGH_ACCURACY) + second_feed_bias
    return block_in + attention_portion + feed_forward_portion

def reference(block_input, ln_gain, norm_layer_bias, query_key_value_weight, query_key_value_bias, attention_output_weight, attention_output_bias, first_feed_weight, first_feed_bias, second_feed_weight, second_feed_bias, cotangent):
    params = tuple((argument.astype(jnp.float32) for argument in (block_input, ln_gain, norm_layer_bias, query_key_value_weight, query_key_value_bias, attention_output_weight, attention_output_bias, first_feed_weight, first_feed_bias, second_feed_weight, second_feed_bias)))
    output, pull = jax.vjp(forward, *params)
    grads = pull(cotangent.astype(jnp.float32))
    bias_grad = grads[4]
    return (output.astype(jnp.bfloat16), grads[0], grads[1], grads[2], grads[3], bias_grad[:2 * D], bias_grad[2 * D:], grads[5], grads[6], grads[7], grads[8], grads[9], grads[10])
```

```python
import functools

import jax
import jax.numpy as jnp
from jax import lax
from jax.experimental import pallas as pl
from jax.experimental.pallas import tpu as pltpu
from jax.sharding import PartitionSpec as P

H = 32
HD = 64
ROT = 32
EPSILON = 1e-05
BOTH = ("fsdp", "seq")
f32 = jnp.float32
bf16 = jnp.bfloat16


def dot(a, b, ca, cb):
    return lax.dot_general(a, b, (((ca,), (cb,)), ((), ())), preferred_element_type=f32)


def causal(tile):
    keys = lax.broadcasted_iota(jnp.int32, tile.shape, 0)
    queries = lax.broadcasted_iota(jnp.int32, tile.shape, 1)
    return jnp.where(queries >= keys, tile, -1e30)


def forward_kernel(block, q_ref, k_ref, v_ref, o_ref, lse_ref, kn_ref):
    blocks = q_ref.shape[1] // block
    kn_ref[...] = k_ref[...].T
    for i in range(blocks):
        rows = pl.ds(i * block, block)
        q = q_ref[:, rows] * jnp.asarray(HD**-0.5, bf16)
        best = total = acc = None
        for j in range(i, -1, -1):
            cols = pl.ds(j * block, block)
            s = dot(kn_ref[cols, :], q, 1, 0)
            if j == i:
                s = causal(s)
            top = jnp.max(s, 0, keepdims=True)
            if best is None:
                best = top
                p = jnp.exp(s - best)
                total = jnp.sum(p, 0, keepdims=True)
                acc = dot(v_ref[:, cols], p.astype(bf16), 1, 0)
            else:
                new = jnp.maximum(best, top)
                fade = jnp.exp(best - new)
                p = jnp.exp(s - new)
                total = total * fade + jnp.sum(p, 0, keepdims=True)
                acc = acc * fade + dot(v_ref[:, cols], p.astype(bf16), 1, 0)
                best = new
        o_ref[:, rows] = (acc / total).astype(bf16)
        lse_ref[0, :, rows] = best + jnp.log(total)


def attend_forward(qkv, heads):
    length = qkv.shape[1]
    block = length // 2

    def spec(part):
        return pl.BlockSpec((HD, length), lambda h: (part * heads + h, 0))

    return pl.pallas_call(
        functools.partial(forward_kernel, block),
        grid=(heads,),
        in_specs=[spec(0), spec(1), spec(2)],
        out_specs=[
            pl.BlockSpec((HD, length), lambda h: (h, 0)),
            pl.BlockSpec((1, 1, length), lambda h: (h, 0, 0)),
        ],
        out_shape=[
            jax.ShapeDtypeStruct((heads * HD, length), bf16),
            jax.ShapeDtypeStruct((heads, 1, length), f32),
        ],
        scratch_shapes=[pltpu.VMEM((length, HD), bf16)],
        compiler_params=pltpu.CompilerParams(vmem_limit_bytes=48 << 20),
        cost_estimate=pl.CostEstimate(
            flops=heads * length * length * 1024, bytes_accessed=length * heads * HD * 8, transcendentals=0
        ),
        name="attend_forward",
    )(qkv, qkv, qkv)


def backward_kernel(block, q_ref, k_ref, v_ref, o_ref, g_ref, lse_ref, d_ref, kn_ref, vn_ref, dk_acc, dv_acc):
    blocks = q_ref.shape[1] // block
    kn_ref[...] = k_ref[...].T
    vn_ref[...] = v_ref[...].T
    for i in range(blocks):
        rows = pl.ds(i * block, block)
        q = q_ref[:, rows] * jnp.asarray(HD**-0.5, bf16)
        g = g_ref[:, rows]
        lse = lse_ref[0, :, rows]
        delta = jnp.sum(g.astype(f32) * o_ref[:, rows].astype(f32), 0, keepdims=True)
        dq = None
        for j in range(i, -1, -1):
            cols = pl.ds(j * block, block)
            s = dot(kn_ref[cols, :], q, 1, 0)
            if j == i:
                s = causal(s)
            p = jnp.exp(s - lse)
            dp = dot(vn_ref[cols, :], g, 1, 0)
            ds = (p * (dp - delta)).astype(bf16)
            dv = dot(g, p.astype(bf16), 1, 1)
            dk = dot(q, ds, 1, 1)
            if j == i:
                dv_acc[:, cols] = dv
                dk_acc[:, cols] = dk
            else:
                dv_acc[:, cols] += dv
                dk_acc[:, cols] += dk
            part = dot(k_ref[:, cols], ds, 1, 0)
            dq = part if dq is None else dq + part
        d_ref[0, 0, :, rows] = (dq * (HD**-0.5)).astype(bf16)
    d_ref[1, 0] = dk_acc[...].astype(bf16)
    d_ref[2, 0] = dv_acc[...].astype(bf16)


def attend_backward(qkv, attn, d_attn, lse, heads):
    length = qkv.shape[1]
    block = length // 4

    def spec(part):
        return pl.BlockSpec((HD, length), lambda h: (part * heads + h, 0))

    return pl.pallas_call(
        functools.partial(backward_kernel, block),
        grid=(heads,),
        in_specs=[
            spec(0),
            spec(1),
            spec(2),
            spec(0),
            spec(0),
            pl.BlockSpec((1, 1, length), lambda h: (h, 0, 0)),
        ],
        out_specs=pl.BlockSpec((3, 1, HD, length), lambda h: (0, h, 0, 0)),
        out_shape=jax.ShapeDtypeStruct((3, heads, HD, length), bf16),
        scratch_shapes=[pltpu.VMEM((length, HD), bf16)] * 2 + [pltpu.VMEM((HD, length), f32)] * 2,
        compiler_params=pltpu.CompilerParams(vmem_limit_bytes=48 << 20),
        cost_estimate=pl.CostEstimate(
            flops=heads * length * length * 2048, bytes_accessed=length * heads * HD * 16, transcendentals=0
        ),
        name="attend_backward",
    )(qkv, qkv, qkv, attn, d_attn, lse)


def normalise(values):
    average = jnp.mean(values, -1, keepdims=True)
    centred = values - average
    variance = jnp.mean(centred * centred, -1, keepdims=True)
    inverse = lax.rsqrt(variance + EPSILON)
    return centred * inverse, inverse


def gelu_tanh(values):
    return 0.5 * values * (1.0 + jnp.tanh(0.7978845608028654 * (values + 0.044715 * values * values * values)))


def rotate(parts, cosine, sine):
    half = ROT // 2
    first, second = parts[..., :half, :], parts[..., half:ROT, :]
    return jnp.concatenate(
        [first * cosine - second * sine, second * cosine + first * sine, parts[..., ROT:, :]], -2
    )


def swap(value, axes, size, bit):
    return lax.ppermute(value, axes, [(i, i ^ bit) for i in range(size)])


def gather_small(values, size):
    index = lax.axis_index(BOTH)
    block = values[None]
    bit = 1
    while bit < size:
        other = swap(block, BOTH, size, bit)
        high = (index & bit) > 0
        block = jnp.concatenate([jnp.where(high, other, block), jnp.where(high, block, other)], 0)
        bit *= 2
    return block


def scatter_small(values, size):
    index = lax.axis_index(BOTH)
    block = values
    bit = size // 2
    while bit:
        high = (index & bit) > 0
        low_half, high_half = block[:bit], block[bit:]
        other = swap(jnp.where(high, low_half, high_half), BOTH, size, bit)
        block = jnp.where(high, high_half, low_half) + other
        bit //= 2
    return block[0]


def gather_tokens(own, groups):
    if groups != 8:
        return lax.all_gather(own, "seq", axis=0, tiled=True)
    index = lax.axis_index("seq")
    core, place = index % 2, index // 2
    by_x = swap(own, "seq", 8, 2)
    by_y = swap(own, "seq", 8, 4)
    relay = jnp.where(core == 0, by_y, by_x)
    diagonal = lax.ppermute(relay, "seq", [(i, i ^ (4 if i % 2 else 2)) for i in range(8)])
    mine = jnp.zeros((4, *own.shape), own.dtype)
    for shift, piece in ((0, own), (1, by_x), (2, by_y), (3, diagonal)):
        mine = lax.dynamic_update_index_in_dim(mine, piece, place ^ shift, 0)
    other = swap(mine, "seq", 8, 1)
    both = jnp.zeros((4, 2, *own.shape), own.dtype)
    both = lax.dynamic_update_index_in_dim(both, mine, core, 1)
    both = lax.dynamic_update_index_in_dim(both, other, 1 - core, 1)
    return both.reshape(groups * own.shape[0], *own.shape[1:])


def take(values, index, axis):
    return lax.dynamic_index_in_dim(values, index, axis, keepdims=False)


def scatter_tokens(terms, groups):
    if groups != 8:
        return lax.psum_scatter(terms, "seq", scatter_dimension=0, tiled=True).astype(f32)
    rows, width = terms.shape[0] // groups, terms.shape[1]
    index = lax.axis_index("seq")
    core, x, y = index % 2, (index // 2) % 2, index // 4
    cells = terms.reshape(2, 2, 2, rows, width)
    got = swap(take(cells, 1 - core, 2), "seq", 8, 1)
    cells = take(cells, core, 2).astype(f32) + got.astype(f32)
    half = width // 2
    left, right = cells[..., :half], cells[..., half:]
    got_left = swap(take(left, 1 - x, 1).astype(bf16), "seq", 8, 2)
    got_right = swap(take(right, 1 - y, 0).astype(bf16), "seq", 8, 4)
    left = take(left, x, 1) + got_left.astype(f32)
    right = take(right, y, 0) + got_right.astype(f32)
    got_left = swap(take(left, 1 - y, 0).astype(bf16), "seq", 8, 4)
    got_right = swap(take(right, 1 - x, 0).astype(bf16), "seq", 8, 2)
    left = take(left, y, 0) + got_left.astype(f32)
    right = take(right, x, 0) + got_right.astype(f32)
    return jnp.concatenate([left, right], -1)


def to_columns(weight, groups):
    rows, blocks, _, width = weight.shape
    sent = weight.transpose(2, 0, 1, 3).reshape(groups * rows, blocks * width)
    return lax.all_to_all(sent, "seq", split_axis=0, concat_axis=0, tiled=True)


def to_rows(grads, groups, blocks):
    rows, width = grads.shape[0] // groups, grads.shape[1] // blocks
    got = lax.all_to_all(grads, "seq", split_axis=0, concat_axis=0, tiled=True)
    return got.reshape(groups, rows, blocks, width).transpose(1, 2, 0, 3)


def local(
    block_input,
    ln_gain,
    norm_layer_bias,
    query_key_value_weight,
    query_key_value_bias,
    attention_output_weight,
    attention_output_bias,
    first_feed_weight,
    first_feed_bias,
    second_feed_weight,
    second_feed_bias,
    cotangent,
):
    shards, groups = lax.axis_size("fsdp"), lax.axis_size("seq")
    size = shards * groups
    me = lax.axis_index("seq")
    _, piece, width = block_input.shape
    length = piece * groups
    heads = H // groups
    rows = query_key_value_weight.shape[0]
    hidden_rows = second_feed_weight.shape[0]
    hidden = shards * hidden_rows
    out_rows = attention_output_weight.shape[0]
    whole_heads = out_rows == HD and heads == shards

    x_own, g_own = block_input[0], cotangent[0]
    x_all = gather_tokens(x_own, groups)
    g_all = gather_tokens(g_own, groups)

    wqkv = to_columns(query_key_value_weight.reshape(rows, 3 * heads, groups, HD), groups)
    wqkv = lax.all_gather(wqkv, "fsdp", axis=0, tiled=True)
    if whole_heads:
        wout = lax.all_gather(attention_output_weight, "fsdp", axis=0, tiled=True)
    else:
        wout = lax.all_gather(attention_output_weight, BOTH, axis=0, tiled=True)
        wout = take(wout.reshape(heads, groups, HD, width), me, 1).reshape(heads * HD, width)
    wfc1 = to_columns(first_feed_weight.reshape(rows, shards, groups, hidden_rows), groups)
    wfc1 = lax.all_gather(wfc1, "fsdp", axis=0, tiled=True)
    wfc2 = lax.all_gather(second_feed_weight, "fsdp", axis=0, tiled=True)

    vectors = (
        ln_gain,
        norm_layer_bias,
        query_key_value_bias,
        attention_output_bias,
        first_feed_bias,
        second_feed_bias,
    )
    small = gather_small(jnp.concatenate(vectors), size).astype(f32)
    pieces, at = [], 0
    for vector in vectors:
        pieces.append(small[:, at : at + vector.shape[0]].reshape(-1))
        at += vector.shape[0]
    gain, shift, bqkv, bout, bfc1, bfc2 = pieces
    bqkv = take(bqkv.reshape(3, heads, groups, HD), me, 2).reshape(-1)
    bfc1 = take(bfc1.reshape(shards, groups, hidden_rows), me, 1).reshape(-1)

    normed_all = (normalise(x_all.astype(f32))[0] * gain + shift).astype(bf16)
    freqs = 10000.0 ** (-2.0 * jnp.arange(ROT // 2).astype(f32) / ROT)
    angles = freqs[:, None] * jnp.arange(length).astype(f32)[None, :]
    cosine, sine = jnp.cos(angles), jnp.sin(angles)
    projected = dot(wqkv, normed_all, 0, 1) + bqkv[:, None]
    projected = projected.reshape(3, heads, HD, length)
    turned = rotate(projected[:2], cosine, sine)
    qkv = jnp.concatenate([turned, projected[2:]], 0).astype(bf16).reshape(3 * heads * HD, length)
    attn, lse = attend_forward(qkv, heads)
    up_pre = dot(wfc1, normed_all, 0, 1) + bfc1[:, None]
    up_value, gelu_pull = jax.vjp(gelu_tanh, up_pre)
    up = up_value.astype(bf16)
    mixed = dot(attn, wout, 0, 0) + dot(up, wfc2, 0, 0)
    mixed = scatter_tokens(mixed.astype(bf16), groups)
    block_output = (x_own.astype(f32) + mixed + bout + bfc2).astype(bf16)

    d_attn = dot(wout, g_all, 1, 1).astype(bf16)
    d_qkv = attend_backward(qkv, attn, d_attn, lse, heads).astype(f32)
    d_turned = rotate(d_qkv[:2], cosine, -sine)
    d_proj = jnp.concatenate([d_turned, d_qkv[2:]], 0).astype(bf16).reshape(3 * heads * HD, length)
    (d_pre,) = gelu_pull(dot(wfc2, g_all, 1, 1))
    d_pre = d_pre.astype(bf16)
    d_normed = dot(d_proj, wqkv, 0, 1) + dot(d_pre, wfc1, 0, 1)
    d_normed = scatter_tokens(d_normed.astype(bf16), groups)
    xhat, inverse = normalise(x_own.astype(f32))
    e = d_normed * gain
    d_x = (e - jnp.mean(e, -1, keepdims=True) - xhat * jnp.mean(e * xhat, -1, keepdims=True)) * inverse
    grad_input = g_own.astype(f32) + d_x

    term_wqkv = dot(normed_all, d_proj, 0, 1).astype(bf16)
    term_wout = dot(attn, g_all, 1, 0)
    term_wfc1 = dot(normed_all, d_pre, 0, 1).astype(bf16)
    term_wfc2 = dot(up, g_all, 1, 0).astype(bf16)
    grad_wqkv = lax.psum_scatter(term_wqkv, "fsdp", scatter_dimension=0, tiled=True)
    grad_wqkv = to_rows(grad_wqkv, groups, 3 * heads).reshape(rows, 3 * H * HD).astype(f32)
    if whole_heads:
        grad_wout = lax.psum_scatter(term_wout.astype(bf16), "fsdp", scatter_dimension=0, tiled=True).astype(f32)
    else:
        mask = (jnp.arange(groups) == me).astype(f32)
        spread = term_wout.reshape(heads, 1, HD, width) * mask[None, :, None, None]
        spread = spread.astype(bf16).reshape(H * HD, width)
        grad_wout = lax.psum_scatter(spread, BOTH, scatter_dimension=0, tiled=True).astype(f32)
    grad_wfc1 = lax.psum_scatter(term_wfc1, "fsdp", scatter_dimension=0, tiled=True)
    grad_wfc1 = to_rows(grad_wfc1, groups, shards).reshape(rows, -1).astype(f32)
    grad_wfc2 = lax.psum_scatter(term_wfc2, "fsdp", scatter_dimension=0, tiled=True).astype(f32)

    here = (jnp.arange(groups) == me).astype(f32)
    term_bqkv = jnp.sum(d_proj.astype(f32), 1).reshape(3 * heads, 1, HD) * here[None, :, None]
    term_bqkv = term_bqkv.reshape(-1)
    term_bfc1 = (jnp.sum(d_pre.astype(f32), 1).reshape(shards, 1, hidden_rows) * here[None, :, None]).reshape(-1)
    terms = (
        jnp.sum(d_normed * xhat, 0),
        jnp.sum(d_normed, 0),
        term_bqkv[: 2 * H * HD],
        term_bqkv[2 * H * HD :],
        jnp.sum(g_own.astype(f32), 0),
        term_bfc1,
    )
    summed = scatter_small(jnp.concatenate([t.reshape(size, -1) for t in terms], 1), size)
    vector_grads, at = [], 0
    for term in terms:
        count = term.shape[0] // size
        vector_grads.append(summed[at : at + count])
        at += count
    grad_gain, grad_shift, grad_bqk, grad_bv, grad_bout, grad_bfc1 = vector_grads
    return (
        block_output[None],
        grad_input[None],
        grad_gain,
        grad_shift,
        grad_wqkv,
        grad_bqk,
        grad_bv,
        grad_wout,
        grad_bout,
        grad_wfc1,
        grad_bfc1,
        grad_wfc2,
        grad_bout,
    )


def solution(mesh):
    tokens, split = P("fsdp", "seq", None), P(BOTH)
    return jax.shard_map(
        local,
        mesh=mesh,
        in_specs=(tokens, *([split] * 10), tokens),
        out_specs=(tokens, tokens, *([split] * 11)),
        check_vma=False,
    )
```

```python
import functools

import jax
import jax.numpy as jnp
from jax import lax
from jax.experimental import pallas as pl
from jax.experimental.pallas import tpu as pltpu
from jax.sharding import PartitionSpec as P

H = 32
HD = 64
ROT = 32
EPSILON = 1e-05
BOTH = ("fsdp", "seq")
f32 = jnp.float32
bf16 = jnp.bfloat16


def dot(a, b, ca, cb):
    return lax.dot_general(a, b, (((ca,), (cb,)), ((), ())), preferred_element_type=f32)


def causal(tile):
    keys = lax.broadcasted_iota(jnp.int32, tile.shape, 0)
    queries = lax.broadcasted_iota(jnp.int32, tile.shape, 1)
    return jnp.where(queries >= keys, tile, -1e30)


def forward_kernel(block, q_ref, k_ref, v_ref, cos_ref, sin_ref, *refs):
    o_ref, lse_ref, qkv_ref, kn_ref = refs[-4:]
    blocks = q_ref.shape[1] // block
    qkv_ref[0, 0] = rotate(q_ref[...], cos_ref[...], sin_ref[...]).astype(bf16)
    turned = rotate(k_ref[...], cos_ref[...], sin_ref[...]).astype(bf16)
    qkv_ref[1, 0] = turned
    kn_ref[...] = turned.T
    qkv_ref[2, 0] = v_ref[...].astype(bf16)
    for i in range(blocks):
        rows = pl.ds(i * block, block)
        q = qkv_ref[0, 0, :, rows] * jnp.asarray(HD**-0.5, bf16)
        best = total = acc = None
        for j in range(i, -1, -1):
            cols = pl.ds(j * block, block)
            s = dot(kn_ref[cols, :], q, 1, 0)
            if j == i:
                s = causal(s)
            top = jnp.max(s, 0, keepdims=True)
            v = qkv_ref[2, 0, :, cols]
            if best is None:
                best = top
                p = jnp.exp(s - best)
                total = jnp.sum(p, 0, keepdims=True)
                acc = dot(v, p.astype(bf16), 1, 0)
            else:
                new = jnp.maximum(best, top)
                fade = jnp.exp(best - new)
                p = jnp.exp(s - new)
                total = total * fade + jnp.sum(p, 0, keepdims=True)
                acc = acc * fade + dot(v, p.astype(bf16), 1, 0)
                best = new
        o_ref[:, rows] = (acc / total).astype(bf16)
        lse_ref[0, :, rows] = best + jnp.log(total)


def attend_forward(projected, cosine, sine, heads, *others):
    length = projected.shape[1]
    block = length // 2

    def spec(part):
        return pl.BlockSpec((HD, length), lambda h: (part * heads + h, 0))

    table = pl.BlockSpec((ROT // 2, length), lambda h: (0, 0))
    return pl.pallas_call(
        functools.partial(forward_kernel, block),
        grid=(heads,),
        in_specs=[spec(0), spec(1), spec(2), table, table] + [pl.BlockSpec(memory_space=pl.ANY)] * len(others),
        out_specs=[
            spec(0),
            pl.BlockSpec((1, 1, length), lambda h: (h, 0, 0)),
            pl.BlockSpec((3, 1, HD, length), lambda h: (0, h, 0, 0)),
        ],
        out_shape=[
            jax.ShapeDtypeStruct((heads * HD, length), bf16),
            jax.ShapeDtypeStruct((heads, 1, length), f32),
            jax.ShapeDtypeStruct((3, heads, HD, length), bf16),
        ],
        scratch_shapes=[pltpu.VMEM((length, HD), bf16)],
        compiler_params=pltpu.CompilerParams(vmem_limit_bytes=48 << 20),
        cost_estimate=pl.CostEstimate(flops=int(1.15e9 * (17)), bytes_accessed=1, transcendentals=0),
        name="attend_forward",
    )(projected, projected, projected, cosine, sine, *others)


def backward_kernel(block, qkv_ref, o_ref, g_ref, lse_ref, cos_ref, sin_ref, *refs):
    d_ref, sum_ref, kn_ref, vn_ref, dk_acc, dv_acc = refs
    blocks = o_ref.shape[1] // block
    kn_ref[...] = qkv_ref[1, 0].T
    vn_ref[...] = qkv_ref[2, 0].T

    def turn_back(values, cols):
        values = values.astype(bf16).astype(f32)
        return rotate(values, cos_ref[:, cols], -sin_ref[:, cols]).astype(bf16)

    for i in range(blocks):
        rows = pl.ds(i * block, block)
        q = qkv_ref[0, 0, :, rows] * jnp.asarray(HD**-0.5, bf16)
        g = g_ref[:, rows]
        lse = lse_ref[0, :, rows]
        delta = jnp.sum(g.astype(f32) * o_ref[:, rows].astype(f32), 0, keepdims=True)
        dq = None
        for j in range(i, -1, -1):
            cols = pl.ds(j * block, block)
            s = dot(kn_ref[cols, :], q, 1, 0)
            if j == i:
                s = causal(s)
            p = jnp.exp(s - lse)
            dp = dot(vn_ref[cols, :], g, 1, 0)
            ds = (p * (dp - delta)).astype(bf16)
            dv = dot(g, p.astype(bf16), 1, 1)
            dk = dot(q, ds, 1, 1)
            if j == i:
                dv_acc[:, cols] = dv
                dk_acc[:, cols] = dk
            else:
                dv_acc[:, cols] += dv
                dk_acc[:, cols] += dk
            part = dot(qkv_ref[1, 0, :, cols], ds, 1, 0)
            dq = part if dq is None else dq + part
        d_ref[0, 0, :, rows] = turn_back(dq * (HD**-0.5), rows)
    d_ref[1, 0] = turn_back(dk_acc[...], pl.ds(0, o_ref.shape[1]))
    d_ref[2, 0] = dv_acc[...].astype(bf16)
    for part in range(3):
        total = jnp.sum(d_ref[part, 0].astype(f32), 1, keepdims=True)
        sum_ref[part, 0] = jnp.broadcast_to(total, sum_ref.shape[2:])


def attend_backward(qkv, attn, d_attn, lse, cosine, sine, heads):
    length = qkv.shape[-1]
    block = length // 4
    one = pl.BlockSpec((HD, length), lambda h: (h, 0))
    three = pl.BlockSpec((3, 1, HD, length), lambda h: (0, h, 0, 0))
    table = pl.BlockSpec((ROT // 2, length), lambda h: (0, 0))
    return pl.pallas_call(
        functools.partial(backward_kernel, block),
        grid=(heads,),
        in_specs=[three, one, one, pl.BlockSpec((1, 1, length), lambda h: (h, 0, 0)), table, table],
        out_specs=[three, pl.BlockSpec((3, 1, HD, 128), lambda h: (0, h, 0, 0))],
        out_shape=[
            jax.ShapeDtypeStruct((3, heads, HD, length), bf16),
            jax.ShapeDtypeStruct((3, heads, HD, 128), f32),
        ],
        scratch_shapes=[pltpu.VMEM((length, HD), bf16)] * 2 + [pltpu.VMEM((HD, length), f32)] * 2,
        compiler_params=pltpu.CompilerParams(vmem_limit_bytes=48 << 20),
        cost_estimate=pl.CostEstimate(flops=int(1.15e9 * (28)), bytes_accessed=1, transcendentals=0),
        name="attend_backward",
    )(qkv, attn, d_attn, lse, cosine, sine)


def back_kernel(turned, core_ref, a_ref, wa_ref, b_ref, wb_ref, *refs):
    send_ref, keep_ref = refs[turned : turned + 2]
    side = 1 if turned else 0
    value = dot(a_ref[...], wa_ref[...], 0, side) + dot(b_ref[...], wb_ref[...], 0, side)
    if turned:
        hat_ref, sums_ref = refs[0], refs[3]

        @pl.when(pl.program_id(0) == 0)
        def _():
            sums_ref[...] = jnp.zeros_like(sums_ref)

        sums_ref[0:1] += jnp.sum(value * hat_ref[...].astype(f32), 0, keepdims=True)
        sums_ref[1:2] += jnp.sum(value, 0, keepdims=True)
    value = value.astype(bf16)
    rows = send_ref.shape[1]
    for core in range(2):

        @pl.when(core_ref[0] == core)
        def _():
            keep_ref[0] = value[core * rows : (core + 1) * rows]
            send_ref[0] = value[(1 - core) * rows : (2 - core) * rows]


def back_product(a, wa, b, wb, groups, hat=None):
    turned = hat is not None
    length, width = a.shape[1], wb.shape[0 if turned else 1]
    places = groups // 2
    block = length // places

    def left(value):
        return pl.BlockSpec((value.shape[0], block), lambda i, core: (0, i))

    def right(value):
        depth = value.shape[0]
        return pl.BlockSpec((width, depth) if turned else (depth, width), lambda i, core: (0, 0))

    half = jax.ShapeDtypeStruct((places, block // 2, width), bf16)
    core = (lax.axis_index("seq") % 2).astype(jnp.int32).reshape(1)
    hats = [hat] if turned else []
    return pl.pallas_call(
        functools.partial(back_kernel, turned),
        grid_spec=pltpu.PrefetchScalarGridSpec(
            num_scalar_prefetch=1,
            grid=(places,),
            in_specs=[left(a), right(a), left(b), right(b)]
            + [pl.BlockSpec((block, width), lambda i, core: (i, 0))] * len(hats),
            out_specs=[pl.BlockSpec((1, block // 2, width), lambda i, core: (i, 0, 0))] * 2
            + [pl.BlockSpec((8, width), lambda i, core: (0, 0))] * len(hats),
        ),
        out_shape=[half, half] + [jax.ShapeDtypeStruct((8, width), f32)] * len(hats),
        compiler_params=pltpu.CompilerParams(vmem_limit_bytes=56 << 20),
        cost_estimate=pl.CostEstimate(flops=int(1.15e9 * (27 if hats else 17)), bytes_accessed=1, transcendentals=0),
        name="back_product",
    )(core, a, wa, b, wb, *hats)


def normalise(values):
    average = jnp.mean(values, -1, keepdims=True)
    centred = values - average
    variance = jnp.mean(centred * centred, -1, keepdims=True)
    inverse = lax.rsqrt(variance + EPSILON)
    return centred * inverse, inverse


def gelu_tanh(values):
    scale, cubic = 0.7978845608028654, 0.044715
    curve = jnp.tanh(scale * (values + cubic * values * values * values))
    slope = 0.5 * (1.0 + curve) + 0.5 * values * (1.0 - curve * curve) * scale * (1.0 + 3.0 * cubic * values * values)
    return 0.5 * values * (1.0 + curve), slope


def rotate(parts, cosine, sine):
    half = ROT // 2
    first, second = parts[..., :half, :], parts[..., half:ROT, :]
    return jnp.concatenate(
        [first * cosine - second * sine, second * cosine + first * sine, parts[..., ROT:, :]], -2
    )


def swap(value, axes, size, bit):
    return lax.ppermute(value, axes, [(i, i ^ bit) for i in range(size)])


def gather_small(values, axis):
    index, count = lax.axis_index(axis), lax.axis_size(axis)
    block, bit = values[None], 1
    while bit < count:
        other = swap(block, axis, count, bit)
        high = (index & bit) > 0
        block = jnp.concatenate([jnp.where(high, other, block), jnp.where(high, block, other)], 0)
        bit *= 2
    return block


def scatter_small(values, size):
    index = lax.axis_index(BOTH)
    block = values
    bit = size // 2
    while bit:
        high = (index & bit) > 0
        low_half, high_half = block[:bit], block[bit:]
        other = swap(jnp.where(high, low_half, high_half), BOTH, size, bit)
        block = jnp.where(high, high_half, low_half) + other
        bit //= 2
    return block[0]


def gate(value, *others):
    anywhere = pl.BlockSpec(memory_space=pl.ANY)
    return pl.pallas_call(
        lambda *refs: None,
        in_specs=[anywhere] * (1 + len(others)),
        out_specs=anywhere,
        out_shape=jax.ShapeDtypeStruct(value.shape, value.dtype),
        input_output_aliases={0: 0},
        name="gate",
    )(value, *others)


def gather_pieces(own, wait=None):
    core = lax.axis_index("seq") % 2
    by_x = swap(own, "seq", 8, 2)
    by_y = swap(own, "seq", 8, 4)
    if wait:
        by_x = gate(by_x, *wait)
    relay = jnp.where(core == 0, by_y, by_x)
    diagonal = lax.ppermute(relay, "seq", [(i, i ^ (4 if i % 2 else 2)) for i in range(8)])
    mine = [own, by_x, by_y, diagonal]
    return [piece for one in mine for piece in (one, swap(one, "seq", 8, 1))]


def pieces_kernel(normed, order_ref, *refs):
    pieces = refs[:8]
    held = refs[-1]
    at = pl.program_id(0)
    for which, piece in enumerate(pieces):

        @pl.when(at == which)
        def _():
            held[...] = piece[...]

    if normed:
        gain_ref, shift_ref = refs[8:10]
        o_ref, hat_ref = refs[10:12]
        for at in range(0, held.shape[0], 32):
            rows = pl.ds(at, 32)
            value = normalise(held[rows, :].astype(f32))[0]
            hat_ref[rows, :] = value.astype(bf16)
            o_ref[rows, :] = (value * gain_ref[...] + shift_ref[...]).astype(bf16)


def put_in_order(pieces, *vectors, after=None):
    index = lax.axis_index("seq")
    order = jnp.stack([index ^ (2 * (which // 2)) ^ (which % 2) for which in range(8)]).astype(jnp.int32)
    rows, width = pieces[0].shape
    vectors = [vector.reshape(1, width) for vector in vectors]
    after = [] if after is None else [after]
    outs = 2 if vectors else 1
    return pl.pallas_call(
        functools.partial(pieces_kernel, bool(vectors)),
        grid_spec=pltpu.PrefetchScalarGridSpec(
            num_scalar_prefetch=1,
            grid=(8,),
            in_specs=[pl.BlockSpec((rows, width), lambda i, order: (0, 0))] * 8
            + [pl.BlockSpec((1, width), lambda i, order: (0, 0))] * len(vectors)
            + [pl.BlockSpec(memory_space=pl.ANY)] * len(after),
            out_specs=[pl.BlockSpec((rows, width), lambda i, order: (order[i], 0))] * outs,
            scratch_shapes=[pltpu.VMEM((rows, width), bf16)] * (len(vectors) > 0),
        ),
        out_shape=[jax.ShapeDtypeStruct((8 * rows, width), bf16)] * outs,
        compiler_params=pltpu.CompilerParams(vmem_limit_bytes=40 << 20),
        cost_estimate=pl.CostEstimate(flops=int(1.15e9 * (10)), bytes_accessed=1, transcendentals=0),
        name="put_in_order",
    )(order, *pieces, *vectors, *after)


def take(values, index, axis):
    return lax.dynamic_index_in_dim(values, index, axis, keepdims=False)


def sum_core(send, keep):
    return keep.astype(f32) + swap(send, "seq", 8, 1).astype(f32)


def sum_sends(cells):
    index = lax.axis_index("seq")
    x, y = (index // 2) % 2, index // 4
    half = cells.shape[2] // 2
    cells = cells.reshape(2, 2, *cells.shape[1:])
    left, right = cells[..., :half], cells[..., half:]
    sends = take(left, 1 - x, 1).astype(bf16), take(right, 1 - y, 0).astype(bf16)
    return sends, (take(left, x, 1), take(right, y, 0))


def sum_start(sends, stays):
    got_left, got_right = swap(sends[0], "seq", 8, 2), swap(sends[1], "seq", 8, 4)
    return stays[0] + got_left.astype(f32), stays[1] + got_right.astype(f32)


def sum_end(left, right):
    index = lax.axis_index("seq")
    x, y = (index // 2) % 2, index // 4
    got_left = swap(take(left, 1 - y, 0).astype(bf16), "seq", 8, 4)
    got_right = swap(take(right, 1 - x, 0).astype(bf16), "seq", 8, 2)
    left = take(left, y, 0) + got_left.astype(f32)
    right = take(right, x, 0) + got_right.astype(f32)
    return jnp.concatenate([left, right], -1)


def spread_kernel(blocks, groups, width, w_ref, o_ref):
    step = max(1, 128 // width)
    for group in range(groups):
        for at in range(0, blocks, step):
            parts = [w_ref[:, pl.ds(((at + k) * groups + group) * width, width)] for k in range(step)]
            o_ref[group, :, pl.ds(at * width, step * width)] = parts[0] if step == 1 else jnp.concatenate(parts, 1)


def collect_kernel(blocks, groups, width, g_ref, o_ref):
    step = max(1, 128 // width)
    for at in range(blocks):
        for group in range(0, groups, step):
            parts = [g_ref[group + k, :, pl.ds(at * width, width)].astype(f32) for k in range(step)]
            where = pl.ds((at * groups + group) * width, step * width)
            o_ref[:, where] = parts[0] if step == 1 else jnp.concatenate(parts, 1)


def local_call(kernel, shape, dtype, *args):
    return pl.pallas_call(
        kernel,
        out_shape=jax.ShapeDtypeStruct(shape, dtype),
        compiler_params=pltpu.CompilerParams(vmem_limit_bytes=32 << 20),
        name="regroup",
    )(*args)


def by_group(weight, blocks, groups):
    rows, width = weight.shape[0], weight.shape[1] // (blocks * groups)
    kernel = functools.partial(spread_kernel, blocks, groups, width)
    out = local_call(kernel, (groups, rows, blocks * width), bf16, weight)
    return out.reshape(groups * rows, blocks * width)


def trade(values):
    return lax.all_to_all(values, "seq", split_axis=0, concat_axis=0, tiled=True)


def to_rows(grads, groups, blocks):
    rows, width = grads.shape[0] // groups, grads.shape[1] // blocks
    got = grads.reshape(groups, rows, blocks * width)
    kernel = functools.partial(collect_kernel, blocks, groups, width)
    return local_call(kernel, (rows, blocks * groups * width), f32, got)


def local(
    block_input,
    ln_gain,
    norm_layer_bias,
    query_key_value_weight,
    query_key_value_bias,
    attention_output_weight,
    attention_output_bias,
    first_feed_weight,
    first_feed_bias,
    second_feed_weight,
    second_feed_bias,
    cotangent,
):
    shards, groups = lax.axis_size("fsdp"), lax.axis_size("seq")
    size = shards * groups
    me = lax.axis_index("seq")
    _, piece, width = block_input.shape
    length = piece * groups
    heads = H // groups
    rows = query_key_value_weight.shape[0]
    hidden_rows = second_feed_weight.shape[0]
    hidden = shards * hidden_rows
    out_rows = attention_output_weight.shape[0]
    whole_heads = out_rows == HD and heads == shards

    x_own, g_own = block_input[0], cotangent[0]
    vectors = (
        ln_gain,
        norm_layer_bias,
        query_key_value_bias,
        attention_output_bias,
        first_feed_bias,
        second_feed_bias,
    )
    small = gather_small(jnp.concatenate(vectors), "fsdp")
    small = gather_small(small, "seq").astype(f32)
    pieces, at = [], 0
    for vector in vectors:
        part = small[:, :, at : at + vector.shape[0]]
        pieces.append(part.transpose(1, 0, 2).reshape(-1))
        at += vector.shape[0]
    gain, shift, bqkv, bout, bfc1, bfc2 = pieces
    bqkv = take(bqkv.reshape(3, heads, groups, HD), me, 2).reshape(-1)
    bfc1 = take(bfc1.reshape(shards, groups, hidden_rows), me, 1).reshape(-1)
    inner = 3 * heads * HD
    wfc2 = lax.all_gather(second_feed_weight, "fsdp", axis=0, tiled=True)
    wfc1 = trade(by_group(first_feed_weight, shards, groups))
    wfc1 = lax.all_gather(gate(wfc1, wfc2), "fsdp", axis=0, tiled=True)
    first = trade(by_group(query_key_value_weight, 3 * heads, groups))
    if whole_heads:
        first = jnp.concatenate([first, attention_output_weight.reshape(groups * rows, -1)], 1)
    first = lax.all_gather(gate(first, wfc1), "fsdp", axis=0, tiled=True)
    if groups == 8:
        x_pieces = gather_pieces(x_own)
        normed_all, hat_all = put_in_order(x_pieces, gain, shift)
        (g_all,) = put_in_order(gather_pieces(gate(g_own, normed_all)))
    else:
        x_all = lax.all_gather(x_own, "seq", axis=0, tiled=True)
        hat_all = normalise(x_all.astype(f32))[0]
        normed_all = (hat_all * gain + shift).astype(bf16)
        g_all = lax.all_gather(g_own, "seq", axis=0, tiled=True)

    up_pre = dot(wfc1, normed_all, 0, 1) + bfc1[:, None]
    up, slope = gelu_tanh(up_pre)
    up = up.astype(bf16)
    term_wfc2 = dot(up, g_all, 1, 0).astype(bf16)
    d_pre = (dot(wfc2, g_all, 1, 1) * slope).astype(bf16)
    term_wfc1 = dot(normed_all, d_pre, 0, 1).astype(bf16)
    folds = width // hidden
    term_wfc1 = jnp.split(term_wfc1.reshape(shards, -1, hidden), folds, 1)
    both = jnp.concatenate([term_wfc2.reshape(shards, -1, width), jnp.concatenate(term_wfc1, 2)], 1)
    both = lax.psum_scatter(both.reshape(-1, width), "fsdp", scatter_dimension=0, tiled=True)
    grad_wfc2 = both[:hidden_rows]
    grad_wfc1 = jnp.concatenate(jnp.split(both[hidden_rows:], folds, 1), 0)

    weights_a = first
    wqkv = first[:, :inner]
    if whole_heads:
        wout = first[:, inner:].reshape(heads * HD, width)
    else:
        wout = lax.all_gather(attention_output_weight, BOTH, axis=0, tiled=True)
        wout = take(wout.reshape(heads, groups, HD, width), me, 1).reshape(heads * HD, width)
    freqs = 10000.0 ** (-2.0 * jnp.arange(ROT // 2).astype(f32) / ROT)
    angles = freqs[:, None] * jnp.arange(length).astype(f32)[None, :]
    cosine, sine = jnp.cos(angles), jnp.sin(angles)
    projected = dot(wqkv, normed_all, 0, 1) + bqkv[:, None]
    attn, lse, qkv = attend_forward(projected, cosine, sine, heads)
    d_attn = dot(wout, g_all, 1, 1).astype(bf16)
    d_proj, sum_proj = attend_backward(qkv, attn, d_attn, lse, cosine, sine, heads)
    d_proj, sum_proj = d_proj.reshape(inner, length), sum_proj[..., 0].reshape(inner)
    term_a = dot(normed_all, d_proj, 0, 1).astype(bf16)
    term_wout = dot(attn, g_all, 1, 0).astype(bf16)
    if whole_heads:
        term_a = jnp.concatenate([term_a, term_wout.reshape(width, -1)], 1)
    else:
        mask = (jnp.arange(groups) == me).astype(bf16)
        spread = term_wout.reshape(heads, 1, HD, width) * mask[None, :, None, None]
        spread = spread.reshape(H * HD, width)
        grad_wout = lax.psum_scatter(spread, BOTH, scatter_dimension=0, tiled=True).astype(f32)
    first = lax.psum_scatter(gate(term_a, both), "fsdp", scatter_dimension=0, tiled=True)

    if groups == 8:
        mixed = back_product(attn, wout, up, wfc2, groups)
        *d_normed, sums = back_product(d_proj, weights_a, d_pre, wfc1, groups, hat_all)
        mixed = sum_end(*sum_start(*sum_sends(sum_core(*mixed))))
        d_normed = sum_end(*sum_start(*sum_sends(sum_core(*d_normed))))
    else:
        mixed = dot(attn, wout, 0, 0) + dot(up, wfc2, 0, 0)
        d_normed = dot(d_proj, wqkv, 0, 1) + dot(d_pre, wfc1, 0, 1)
        sums = jnp.stack([jnp.sum(d_normed * hat_all, 0), jnp.sum(d_normed, 0)])
        d_normed, mixed = (
            lax.psum_scatter(v.astype(bf16), "seq", scatter_dimension=0, tiled=True).astype(f32)
            for v in (d_normed, mixed)
        )
    traded = trade(grad_wfc1)
    rows_wfc1 = to_rows(traded, groups, shards)
    grad_wfc2 = grad_wfc2.astype(f32)

    here = (jnp.arange(groups) == me).astype(f32)
    term_bqkv = sum_proj.reshape(3 * heads, 1, HD) * here[None, :, None]
    term_bqkv = term_bqkv.reshape(-1)
    term_bfc1 = (jnp.sum(d_pre.astype(f32), 1).reshape(shards, 1, hidden_rows) * here[None, :, None]).reshape(-1)
    terms = (
        sums[0],
        sums[1],
        term_bqkv[: 2 * H * HD],
        term_bqkv[2 * H * HD :],
        jnp.sum(g_own.astype(f32), 0),
        term_bfc1,
    )
    summed = jnp.concatenate([t.reshape(size, -1) for t in terms], 1)
    summed = scatter_small(summed, size)
    vector_grads, at = [], 0
    for term in terms:
        count = term.shape[0] // size
        vector_grads.append(summed[at : at + count])
        at += count
    grad_gain, grad_shift, grad_bqk, grad_bv, grad_bout, grad_bfc1 = vector_grads

    first = gate(first, d_normed, mixed, traded, summed)
    if whole_heads:
        grad_wout = first[:, inner:].reshape(out_rows, width).astype(f32)
    grad_wqkv = to_rows(trade(first[:, :inner]), groups, 3 * heads)
    block_output = (x_own.astype(f32) + mixed + bout + bfc2).astype(bf16)
    xhat, inverse = normalise(x_own.astype(f32))
    e = d_normed * gain
    d_x = (e - jnp.mean(e, -1, keepdims=True) - xhat * jnp.mean(e * xhat, -1, keepdims=True)) * inverse
    grad_input = g_own.astype(f32) + d_x
    return (
        block_output[None],
        grad_input[None],
        grad_gain,
        grad_shift,
        grad_wqkv,
        grad_bqk,
        grad_bv,
        grad_wout,
        grad_bout,
        rows_wfc1,
        grad_bfc1,
        grad_wfc2,
        grad_bout,
    )


def solution(mesh):
    tokens, split = P("fsdp", "seq", None), P(BOTH)
    return jax.shard_map(
        local,
        mesh=mesh,
        in_specs=(tokens, *([split] * 10), tokens),
        out_specs=(tokens, tokens, *([split] * 11)),
        check_vma=False,
    )
```

```python
import functools

import jax
import jax.numpy as jnp
from jax import lax
from jax.experimental import pallas as pl
from jax.experimental.pallas import tpu as pltpu
from jax.sharding import PartitionSpec as P

H = 32
HD = 64
ROT = 32
EPSILON = 1e-05
BOTH = ("fsdp", "seq")
f32 = jnp.float32
bf16 = jnp.bfloat16


def dot(a, b, ca, cb):
    return lax.dot_general(a, b, (((ca,), (cb,)), ((), ())), preferred_element_type=f32)


def causal(tile):
    keys = lax.broadcasted_iota(jnp.int32, tile.shape, 0)
    queries = lax.broadcasted_iota(jnp.int32, tile.shape, 1)
    return jnp.where(queries >= keys, tile, -1e30)


def forward_kernel(block, q_ref, k_ref, v_ref, cos_ref, sin_ref, *refs):
    o_ref, lse_ref, qkv_ref, kn_ref = refs[-4:]
    blocks = q_ref.shape[1] // block
    qkv_ref[0, 0] = rotate(q_ref[...], cos_ref[...], sin_ref[...]).astype(bf16)
    turned = rotate(k_ref[...], cos_ref[...], sin_ref[...]).astype(bf16)
    qkv_ref[1, 0] = turned
    kn_ref[...] = turned.T
    qkv_ref[2, 0] = v_ref[...].astype(bf16)
    for i in range(blocks):
        rows = pl.ds(i * block, block)
        q = qkv_ref[0, 0, :, rows] * jnp.asarray(HD**-0.5, bf16)
        best = total = acc = None
        for j in range(i, -1, -1):
            cols = pl.ds(j * block, block)
            s = dot(kn_ref[cols, :], q, 1, 0)
            if j == i:
                s = causal(s)
            top = jnp.max(s, 0, keepdims=True)
            v = qkv_ref[2, 0, :, cols]
            if best is None:
                best = top
                p = jnp.exp(s - best)
                total = jnp.sum(p, 0, keepdims=True)
                acc = dot(v, p.astype(bf16), 1, 0)
            else:
                new = jnp.maximum(best, top)
                fade = jnp.exp(best - new)
                p = jnp.exp(s - new)
                total = total * fade + jnp.sum(p, 0, keepdims=True)
                acc = acc * fade + dot(v, p.astype(bf16), 1, 0)
                best = new
        o_ref[:, rows] = (acc / total).astype(bf16)
        lse_ref[0, :, rows] = best + jnp.log(total)


def attend_forward(projected, cosine, sine, heads, *others):
    length = projected.shape[1]
    block = length // 2

    def spec(part):
        return pl.BlockSpec((HD, length), lambda h: (part * heads + h, 0))

    table = pl.BlockSpec((ROT // 2, length), lambda h: (0, 0))
    return pl.pallas_call(
        functools.partial(forward_kernel, block),
        grid=(heads,),
        in_specs=[spec(0), spec(1), spec(2), table, table] + [pl.BlockSpec(memory_space=pl.ANY)] * len(others),
        out_specs=[
            spec(0),
            pl.BlockSpec((1, 1, length), lambda h: (h, 0, 0)),
            pl.BlockSpec((3, 1, HD, length), lambda h: (0, h, 0, 0)),
        ],
        out_shape=[
            jax.ShapeDtypeStruct((heads * HD, length), bf16),
            jax.ShapeDtypeStruct((heads, 1, length), f32),
            jax.ShapeDtypeStruct((3, heads, HD, length), bf16),
        ],
        scratch_shapes=[pltpu.VMEM((length, HD), bf16)],
        compiler_params=pltpu.CompilerParams(vmem_limit_bytes=48 << 20),
        cost_estimate=pl.CostEstimate(flops=int(1.15e9 * (17)), bytes_accessed=1, transcendentals=0),
        name="attend_forward",
    )(projected, projected, projected, cosine, sine, *others)


def backward_kernel(block, qkv_ref, o_ref, g_ref, lse_ref, cos_ref, sin_ref, *refs):
    d_ref, sum_ref, kn_ref, vn_ref, dk_acc, dv_acc = refs
    blocks = o_ref.shape[1] // block
    kn_ref[...] = qkv_ref[1, 0].T
    vn_ref[...] = qkv_ref[2, 0].T

    def turn_back(values, cols):
        values = values.astype(bf16).astype(f32)
        return rotate(values, cos_ref[:, cols], -sin_ref[:, cols]).astype(bf16)

    for i in range(blocks):
        rows = pl.ds(i * block, block)
        q = qkv_ref[0, 0, :, rows] * jnp.asarray(HD**-0.5, bf16)
        g = g_ref[:, rows]
        lse = lse_ref[0, :, rows]
        delta = jnp.sum(g.astype(f32) * o_ref[:, rows].astype(f32), 0, keepdims=True)
        dq = None
        for j in range(i, -1, -1):
            cols = pl.ds(j * block, block)
            s = dot(kn_ref[cols, :], q, 1, 0)
            if j == i:
                s = causal(s)
            p = jnp.exp(s - lse)
            dp = dot(vn_ref[cols, :], g, 1, 0)
            ds = (p * (dp - delta)).astype(bf16)
            dv = dot(g, p.astype(bf16), 1, 1)
            dk = dot(q, ds, 1, 1)
            if j == i:
                dv_acc[:, cols] = dv
                dk_acc[:, cols] = dk
            else:
                dv_acc[:, cols] += dv
                dk_acc[:, cols] += dk
            part = dot(qkv_ref[1, 0, :, cols], ds, 1, 0)
            dq = part if dq is None else dq + part
        d_ref[0, 0, :, rows] = turn_back(dq * (HD**-0.5), rows)
    d_ref[1, 0] = turn_back(dk_acc[...], pl.ds(0, o_ref.shape[1]))
    d_ref[2, 0] = dv_acc[...].astype(bf16)
    for part in range(3):
        total = jnp.sum(d_ref[part, 0].astype(f32), 1, keepdims=True)
        sum_ref[part, 0] = jnp.broadcast_to(total, sum_ref.shape[2:])


def attend_backward(qkv, attn, d_attn, lse, cosine, sine, heads):
    length = qkv.shape[-1]
    block = length // 4
    one = pl.BlockSpec((HD, length), lambda h: (h, 0))
    three = pl.BlockSpec((3, 1, HD, length), lambda h: (0, h, 0, 0))
    table = pl.BlockSpec((ROT // 2, length), lambda h: (0, 0))
    return pl.pallas_call(
        functools.partial(backward_kernel, block),
        grid=(heads,),
        in_specs=[three, one, one, pl.BlockSpec((1, 1, length), lambda h: (h, 0, 0)), table, table],
        out_specs=[three, pl.BlockSpec((3, 1, HD, 128), lambda h: (0, h, 0, 0))],
        out_shape=[
            jax.ShapeDtypeStruct((3, heads, HD, length), bf16),
            jax.ShapeDtypeStruct((3, heads, HD, 128), f32),
        ],
        scratch_shapes=[pltpu.VMEM((length, HD), bf16)] * 2 + [pltpu.VMEM((HD, length), f32)] * 2,
        compiler_params=pltpu.CompilerParams(vmem_limit_bytes=48 << 20),
        cost_estimate=pl.CostEstimate(flops=int(1.15e9 * (28)), bytes_accessed=1, transcendentals=0),
        name="attend_backward",
    )(qkv, attn, d_attn, lse, cosine, sine)


def back_kernel(turned, core_ref, a_ref, wa_ref, b_ref, wb_ref, *refs):
    send_ref, keep_ref = refs[turned : turned + 2]
    side = 1 if turned else 0
    value = dot(a_ref[...], wa_ref[...], 0, side) + dot(b_ref[...], wb_ref[...], 0, side)
    if turned:
        hat_ref, sums_ref = refs[0], refs[3]

        @pl.when(pl.program_id(0) == 0)
        def _():
            sums_ref[...] = jnp.zeros_like(sums_ref)

        sums_ref[0:1] += jnp.sum(value * hat_ref[...].astype(f32), 0, keepdims=True)
        sums_ref[1:2] += jnp.sum(value, 0, keepdims=True)
    value = value.astype(bf16)
    rows = send_ref.shape[1]
    for core in range(2):

        @pl.when(core_ref[0] == core)
        def _():
            keep_ref[0] = value[core * rows : (core + 1) * rows]
            send_ref[0] = value[(1 - core) * rows : (2 - core) * rows]


def back_product(a, wa, b, wb, groups, hat=None):
    turned = hat is not None
    length, width = a.shape[1], wb.shape[0 if turned else 1]
    places = groups // 2
    block = length // places

    def left(value):
        return pl.BlockSpec((value.shape[0], block), lambda i, core: (0, i))

    def right(value):
        depth = value.shape[0]
        return pl.BlockSpec((width, depth) if turned else (depth, width), lambda i, core: (0, 0))

    half = jax.ShapeDtypeStruct((places, block // 2, width), bf16)
    core = (lax.axis_index("seq") % 2).astype(jnp.int32).reshape(1)
    hats = [hat] if turned else []
    return pl.pallas_call(
        functools.partial(back_kernel, turned),
        grid_spec=pltpu.PrefetchScalarGridSpec(
            num_scalar_prefetch=1,
            grid=(places,),
            in_specs=[left(a), right(a), left(b), right(b)]
            + [pl.BlockSpec((block, width), lambda i, core: (i, 0))] * len(hats),
            out_specs=[pl.BlockSpec((1, block // 2, width), lambda i, core: (i, 0, 0))] * 2
            + [pl.BlockSpec((8, width), lambda i, core: (0, 0))] * len(hats),
        ),
        out_shape=[half, half] + [jax.ShapeDtypeStruct((8, width), f32)] * len(hats),
        compiler_params=pltpu.CompilerParams(vmem_limit_bytes=56 << 20),
        cost_estimate=pl.CostEstimate(flops=int(1.15e9 * (27 if hats else 17)), bytes_accessed=1, transcendentals=0),
        name="back_product",
    )(core, a, wa, b, wb, *hats)


def normalise(values):
    average = jnp.mean(values, -1, keepdims=True)
    centred = values - average
    variance = jnp.mean(centred * centred, -1, keepdims=True)
    inverse = lax.rsqrt(variance + EPSILON)
    return centred * inverse, inverse


def gelu_tanh(values):
    scale, cubic = 0.7978845608028654, 0.044715
    curve = jnp.tanh(scale * (values + cubic * values * values * values))
    slope = 0.5 * (1.0 + curve) + 0.5 * values * (1.0 - curve * curve) * scale * (1.0 + 3.0 * cubic * values * values)
    return 0.5 * values * (1.0 + curve), slope


def rotate(parts, cosine, sine):
    half = ROT // 2
    first, second = parts[..., :half, :], parts[..., half:ROT, :]
    return jnp.concatenate(
        [first * cosine - second * sine, second * cosine + first * sine, parts[..., ROT:, :]], -2
    )


def swap(value, axes, size, bit):
    return lax.ppermute(value, axes, [(i, i ^ bit) for i in range(size)])


def gather_small(values, axis):
    index, count = lax.axis_index(axis), lax.axis_size(axis)
    block, bit = values[None], 1
    while bit < count:
        other = swap(block, axis, count, bit)
        high = (index & bit) > 0
        block = jnp.concatenate([jnp.where(high, other, block), jnp.where(high, block, other)], 0)
        bit *= 2
    return block


def scatter_small(values, size):
    index = lax.axis_index(BOTH)
    block = values
    bit = size // 2
    while bit:
        high = (index & bit) > 0
        low_half, high_half = block[:bit], block[bit:]
        other = swap(jnp.where(high, low_half, high_half), BOTH, size, bit)
        block = jnp.where(high, high_half, low_half) + other
        bit //= 2
    return block[0]


def gate(value, *others):
    anywhere = pl.BlockSpec(memory_space=pl.ANY)
    return pl.pallas_call(
        lambda *refs: None,
        in_specs=[anywhere] * (1 + len(others)),
        out_specs=anywhere,
        out_shape=jax.ShapeDtypeStruct(value.shape, value.dtype),
        input_output_aliases={0: 0},
        name="gate",
    )(value, *others)


def gather_pieces(own, wait=None):
    core = lax.axis_index("seq") % 2
    by_x = swap(own, "seq", 8, 2)
    by_y = swap(own, "seq", 8, 4)
    if wait:
        by_x = gate(by_x, *wait)
    relay = jnp.where(core == 0, by_y, by_x)
    diagonal = lax.ppermute(relay, "seq", [(i, i ^ (4 if i % 2 else 2)) for i in range(8)])
    mine = [own, by_x, by_y, diagonal]
    return [piece for one in mine for piece in (one, swap(one, "seq", 8, 1))]


def pieces_kernel(normed, order_ref, *refs):
    pieces = refs[:8]
    held = refs[-1]
    at = pl.program_id(0)
    for which, piece in enumerate(pieces):

        @pl.when(at == which)
        def _():
            held[...] = piece[...]

    if normed:
        gain_ref, shift_ref = refs[8:10]
        o_ref, hat_ref = refs[10:12]
        for at in range(0, held.shape[0], 32):
            rows = pl.ds(at, 32)
            value = normalise(held[rows, :].astype(f32))[0]
            hat_ref[rows, :] = value.astype(bf16)
            o_ref[rows, :] = (value * gain_ref[...] + shift_ref[...]).astype(bf16)


def put_in_order(pieces, *vectors, after=None):
    index = lax.axis_index("seq")
    order = jnp.stack([index ^ (2 * (which // 2)) ^ (which % 2) for which in range(8)]).astype(jnp.int32)
    rows, width = pieces[0].shape
    vectors = [vector.reshape(1, width) for vector in vectors]
    after = [] if after is None else [after]
    outs = 2 if vectors else 1
    return pl.pallas_call(
        functools.partial(pieces_kernel, bool(vectors)),
        grid_spec=pltpu.PrefetchScalarGridSpec(
            num_scalar_prefetch=1,
            grid=(8,),
            in_specs=[pl.BlockSpec((rows, width), lambda i, order: (0, 0))] * 8
            + [pl.BlockSpec((1, width), lambda i, order: (0, 0))] * len(vectors)
            + [pl.BlockSpec(memory_space=pl.ANY)] * len(after),
            out_specs=[pl.BlockSpec((rows, width), lambda i, order: (order[i], 0))] * outs,
            scratch_shapes=[pltpu.VMEM((rows, width), bf16)] * (len(vectors) > 0),
        ),
        out_shape=[jax.ShapeDtypeStruct((8 * rows, width), bf16)] * outs,
        compiler_params=pltpu.CompilerParams(vmem_limit_bytes=40 << 20),
        cost_estimate=pl.CostEstimate(flops=int(1.15e9 * (10)), bytes_accessed=1, transcendentals=0),
        name="put_in_order",
    )(order, *pieces, *vectors, *after)


def take(values, index, axis):
    return lax.dynamic_index_in_dim(values, index, axis, keepdims=False)


def sum_core(send, keep):
    return keep.astype(f32) + swap(send, "seq", 8, 1).astype(f32)


def sum_sends(cells):
    index = lax.axis_index("seq")
    x, y = (index // 2) % 2, index // 4
    half = cells.shape[2] // 2
    cells = cells.reshape(2, 2, *cells.shape[1:])
    left, right = cells[..., :half], cells[..., half:]
    sends = take(left, 1 - x, 1).astype(bf16), take(right, 1 - y, 0).astype(bf16)
    return sends, (take(left, x, 1), take(right, y, 0))


def sum_start(sends, stays):
    got_left, got_right = swap(sends[0], "seq", 8, 2), swap(sends[1], "seq", 8, 4)
    return stays[0] + got_left.astype(f32), stays[1] + got_right.astype(f32)


def sum_end(left, right):
    index = lax.axis_index("seq")
    x, y = (index // 2) % 2, index // 4
    got_left = swap(take(left, 1 - y, 0).astype(bf16), "seq", 8, 4)
    got_right = swap(take(right, 1 - x, 0).astype(bf16), "seq", 8, 2)
    left = take(left, y, 0) + got_left.astype(f32)
    right = take(right, x, 0) + got_right.astype(f32)
    return jnp.concatenate([left, right], -1)


def spread_kernel(blocks, groups, width, w_ref, o_ref):
    step = max(1, 128 // width)
    for group in range(groups):
        for at in range(0, blocks, step):
            parts = [w_ref[:, pl.ds(((at + k) * groups + group) * width, width)] for k in range(step)]
            o_ref[group, :, pl.ds(at * width, step * width)] = parts[0] if step == 1 else jnp.concatenate(parts, 1)


def collect_kernel(blocks, groups, width, g_ref, o_ref):
    step = max(1, 128 // width)
    for at in range(blocks):
        for group in range(0, groups, step):
            parts = [g_ref[group + k, :, pl.ds(at * width, width)].astype(f32) for k in range(step)]
            where = pl.ds((at * groups + group) * width, step * width)
            o_ref[:, where] = parts[0] if step == 1 else jnp.concatenate(parts, 1)


def local_call(kernel, shape, dtype, *args):
    return pl.pallas_call(
        kernel,
        out_shape=jax.ShapeDtypeStruct(shape, dtype),
        compiler_params=pltpu.CompilerParams(vmem_limit_bytes=32 << 20),
        name="regroup",
    )(*args)


def by_group(weight, blocks, groups):
    rows, width = weight.shape[0], weight.shape[1] // (blocks * groups)
    kernel = functools.partial(spread_kernel, blocks, groups, width)
    out = local_call(kernel, (groups, rows, blocks * width), bf16, weight)
    return out.reshape(groups * rows, blocks * width)


def trade(values):
    return lax.all_to_all(values, "seq", split_axis=0, concat_axis=0, tiled=True)


def to_rows(grads, groups, blocks):
    rows, width = grads.shape[0] // groups, grads.shape[1] // blocks
    got = grads.reshape(groups, rows, blocks * width)
    kernel = functools.partial(collect_kernel, blocks, groups, width)
    return local_call(kernel, (rows, blocks * groups * width), f32, got)


def local(
    block_input,
    ln_gain,
    norm_layer_bias,
    query_key_value_weight,
    query_key_value_bias,
    attention_output_weight,
    attention_output_bias,
    first_feed_weight,
    first_feed_bias,
    second_feed_weight,
    second_feed_bias,
    cotangent,
):
    shards, groups = lax.axis_size("fsdp"), lax.axis_size("seq")
    size = shards * groups
    me = lax.axis_index("seq")
    _, piece, width = block_input.shape
    length = piece * groups
    heads = H // groups
    rows = query_key_value_weight.shape[0]
    hidden_rows = second_feed_weight.shape[0]
    hidden = shards * hidden_rows
    out_rows = attention_output_weight.shape[0]
    whole_heads = out_rows == HD and heads == shards

    x_own, g_own = block_input[0], cotangent[0]
    vectors = (
        ln_gain,
        norm_layer_bias,
        query_key_value_bias,
        attention_output_bias,
        first_feed_bias,
        second_feed_bias,
    )
    small = gather_small(jnp.concatenate(vectors), "fsdp")
    small = gather_small(small, "seq").astype(f32)
    pieces, at = [], 0
    for vector in vectors:
        part = small[:, :, at : at + vector.shape[0]]
        pieces.append(part.transpose(1, 0, 2).reshape(-1))
        at += vector.shape[0]
    gain, shift, bqkv, bout, bfc1, bfc2 = pieces
    bqkv = take(bqkv.reshape(3, heads, groups, HD), me, 2).reshape(-1)
    bfc1 = take(bfc1.reshape(shards, groups, hidden_rows), me, 1).reshape(-1)
    inner = 3 * heads * HD
    wfc2 = lax.all_gather(second_feed_weight, "fsdp", axis=0, tiled=True)
    wfc1 = trade(by_group(first_feed_weight, shards, groups))
    wfc1 = lax.all_gather(gate(wfc1, wfc2), "fsdp", axis=0, tiled=True)
    first = trade(by_group(query_key_value_weight, 3 * heads, groups))
    if whole_heads:
        first = jnp.concatenate([first, attention_output_weight.reshape(groups * rows, -1)], 1)
    first = lax.all_gather(gate(first, wfc1), "fsdp", axis=0, tiled=True)
    if groups == 8:
        x_pieces = gather_pieces(x_own)
        normed_all, hat_all = put_in_order(x_pieces, gain, shift)
        (g_all,) = put_in_order(gather_pieces(gate(g_own, normed_all)))
    else:
        x_all = lax.all_gather(x_own, "seq", axis=0, tiled=True)
        hat_all = normalise(x_all.astype(f32))[0]
        normed_all = (hat_all * gain + shift).astype(bf16)
        g_all = lax.all_gather(g_own, "seq", axis=0, tiled=True)

    up_pre = dot(wfc1, normed_all, 0, 1) + bfc1[:, None]
    up, slope = gelu_tanh(up_pre)
    up = up.astype(bf16)
    term_wfc2 = dot(up, g_all, 1, 0).astype(bf16)
    d_pre = (dot(wfc2, g_all, 1, 1) * slope).astype(bf16)
    term_wfc1 = dot(normed_all, d_pre, 0, 1).astype(bf16)
    folds = width // hidden
    term_wfc1 = jnp.split(term_wfc1.reshape(shards, -1, hidden), folds, 1)
    both = jnp.concatenate([term_wfc2.reshape(shards, -1, width), jnp.concatenate(term_wfc1, 2)], 1)
    both = lax.psum_scatter(both.reshape(-1, width), "fsdp", scatter_dimension=0, tiled=True)
    grad_wfc2 = both[:hidden_rows]
    grad_wfc1 = jnp.concatenate(jnp.split(both[hidden_rows:], folds, 1), 0)

    weights_a = first
    wqkv = first[:, :inner]
    if whole_heads:
        wout = first[:, inner:].reshape(heads * HD, width)
    else:
        wout = lax.all_gather(attention_output_weight, BOTH, axis=0, tiled=True)
        wout = take(wout.reshape(heads, groups, HD, width), me, 1).reshape(heads * HD, width)
    freqs = 10000.0 ** (-2.0 * jnp.arange(ROT // 2).astype(f32) / ROT)
    angles = freqs[:, None] * jnp.arange(length).astype(f32)[None, :]
    cosine, sine = jnp.cos(angles), jnp.sin(angles)
    projected = dot(wqkv, normed_all, 0, 1) + bqkv[:, None]
    attn, lse, qkv = attend_forward(projected, cosine, sine, heads)
    d_attn = dot(wout, g_all, 1, 1).astype(bf16)
    d_proj, sum_proj = attend_backward(qkv, attn, d_attn, lse, cosine, sine, heads)
    d_proj, sum_proj = d_proj.reshape(inner, length), sum_proj[..., 0].reshape(inner)
    term_a = dot(normed_all, d_proj, 0, 1).astype(bf16)
    term_wout = dot(attn, g_all, 1, 0).astype(bf16)
    if whole_heads:
        term_a = jnp.concatenate([term_a, term_wout.reshape(width, -1)], 1)
    else:
        mask = (jnp.arange(groups) == me).astype(bf16)
        spread = term_wout.reshape(heads, 1, HD, width) * mask[None, :, None, None]
        spread = spread.reshape(H * HD, width)
        grad_wout = lax.psum_scatter(spread, BOTH, scatter_dimension=0, tiled=True).astype(f32)
    first = lax.psum_scatter(gate(term_a, both), "fsdp", scatter_dimension=0, tiled=True)

    traded = trade(grad_wfc1)
    if groups == 8:
        mixed = back_product(attn, wout, up, wfc2, groups)
        *d_normed, sums = back_product(d_proj, weights_a, d_pre, wfc1, groups, hat_all)
        mixed = sum_end(*sum_start(*sum_sends(sum_core(mixed[0], gate(mixed[1], traded)))))
        d_normed = sum_end(*sum_start(*sum_sends(sum_core(*d_normed))))
    else:
        mixed = dot(attn, wout, 0, 0) + dot(up, wfc2, 0, 0)
        d_normed = dot(d_proj, wqkv, 0, 1) + dot(d_pre, wfc1, 0, 1)
        sums = jnp.stack([jnp.sum(d_normed * hat_all, 0), jnp.sum(d_normed, 0)])
        d_normed, mixed = (
            lax.psum_scatter(v.astype(bf16), "seq", scatter_dimension=0, tiled=True).astype(f32)
            for v in (d_normed, mixed)
        )
    rows_wfc1 = to_rows(traded, groups, shards)
    grad_wfc2 = grad_wfc2.astype(f32)

    here = (jnp.arange(groups) == me).astype(f32)
    term_bqkv = sum_proj.reshape(3 * heads, 1, HD) * here[None, :, None]
    term_bqkv = term_bqkv.reshape(-1)
    term_bfc1 = (jnp.sum(d_pre.astype(f32), 1).reshape(shards, 1, hidden_rows) * here[None, :, None]).reshape(-1)
    terms = (
        sums[0],
        sums[1],
        term_bqkv[: 2 * H * HD],
        term_bqkv[2 * H * HD :],
        jnp.sum(g_own.astype(f32), 0),
        term_bfc1,
    )
    summed = jnp.concatenate([t.reshape(size, -1) for t in terms], 1)
    summed = scatter_small(summed, size)
    vector_grads, at = [], 0
    for term in terms:
        count = term.shape[0] // size
        vector_grads.append(summed[at : at + count])
        at += count
    grad_gain, grad_shift, grad_bqk, grad_bv, grad_bout, grad_bfc1 = vector_grads

    first = gate(first, d_normed)
    if whole_heads:
        grad_wout = first[:, inner:].reshape(out_rows, width).astype(f32)
    grad_wqkv = to_rows(trade(first[:, :inner]), groups, 3 * heads)
    block_output = (x_own.astype(f32) + mixed + bout + bfc2).astype(bf16)
    xhat, inverse = normalise(x_own.astype(f32))
    e = d_normed * gain
    d_x = (e - jnp.mean(e, -1, keepdims=True) - xhat * jnp.mean(e * xhat, -1, keepdims=True)) * inverse
    grad_input = g_own.astype(f32) + d_x
    return (
        block_output[None],
        grad_input[None],
        grad_gain,
        grad_shift,
        grad_wqkv,
        grad_bqk,
        grad_bv,
        grad_wout,
        grad_bout,
        rows_wfc1,
        grad_bfc1,
        grad_wfc2,
        grad_bout,
    )


def solution(mesh):
    tokens, split = P("fsdp", "seq", None), P(BOTH)
    return jax.shard_map(
        local,
        mesh=mesh,
        in_specs=(tokens, *([split] * 10), tokens),
        out_specs=(tokens, tokens, *([split] * 11)),
        check_vma=False,
    )
```

```python
import functools

import jax
import jax.numpy as jnp
from jax import lax
from jax.experimental import pallas as pl
from jax.experimental.pallas import tpu as pltpu
from jax.sharding import PartitionSpec as P

H = 32
HD = 64
ROT = 32
EPSILON = 1e-05
BOTH = ("fsdp", "seq")
f32 = jnp.float32
bf16 = jnp.bfloat16


def dot(a, b, ca, cb):
    return lax.dot_general(a, b, (((ca,), (cb,)), ((), ())), preferred_element_type=f32)


def causal(tile):
    keys = lax.broadcasted_iota(jnp.int32, tile.shape, 0)
    queries = lax.broadcasted_iota(jnp.int32, tile.shape, 1)
    return jnp.where(queries >= keys, tile, -1e30)


def forward_kernel(block, q_ref, k_ref, v_ref, cos_ref, sin_ref, *refs):
    o_ref, lse_ref, qkv_ref, kn_ref = refs[-4:]
    blocks = q_ref.shape[1] // block
    qkv_ref[0, 0] = rotate(q_ref[...], cos_ref[...], sin_ref[...]).astype(bf16)
    turned = rotate(k_ref[...], cos_ref[...], sin_ref[...]).astype(bf16)
    qkv_ref[1, 0] = turned
    kn_ref[...] = turned.T
    qkv_ref[2, 0] = v_ref[...].astype(bf16)
    for i in range(blocks):
        rows = pl.ds(i * block, block)
        q = qkv_ref[0, 0, :, rows] * jnp.asarray(HD**-0.5, bf16)
        best = total = acc = None
        for j in range(i, -1, -1):
            cols = pl.ds(j * block, block)
            s = dot(kn_ref[cols, :], q, 1, 0)
            if j == i:
                s = causal(s)
            top = jnp.max(s, 0, keepdims=True)
            v = qkv_ref[2, 0, :, cols]
            if best is None:
                best = top
                p = jnp.exp(s - best)
                total = jnp.sum(p, 0, keepdims=True)
                acc = dot(v, p.astype(bf16), 1, 0)
            else:
                new = jnp.maximum(best, top)
                fade = jnp.exp(best - new)
                p = jnp.exp(s - new)
                total = total * fade + jnp.sum(p, 0, keepdims=True)
                acc = acc * fade + dot(v, p.astype(bf16), 1, 0)
                best = new
        o_ref[:, rows] = (acc / total).astype(bf16)
        lse_ref[0, :, rows] = best + jnp.log(total)


def attend_forward(projected, cosine, sine, heads, *others):
    length = projected.shape[1]
    block = length // 2

    def spec(part):
        return pl.BlockSpec((HD, length), lambda h: (part * heads + h, 0))

    table = pl.BlockSpec((ROT // 2, length), lambda h: (0, 0))
    return pl.pallas_call(
        functools.partial(forward_kernel, block),
        grid=(heads,),
        in_specs=[spec(0), spec(1), spec(2), table, table] + [pl.BlockSpec(memory_space=pl.ANY)] * len(others),
        out_specs=[
            spec(0),
            pl.BlockSpec((1, 1, length), lambda h: (h, 0, 0)),
            pl.BlockSpec((3, 1, HD, length), lambda h: (0, h, 0, 0)),
        ],
        out_shape=[
            jax.ShapeDtypeStruct((heads * HD, length), bf16),
            jax.ShapeDtypeStruct((heads, 1, length), f32),
            jax.ShapeDtypeStruct((3, heads, HD, length), bf16),
        ],
        scratch_shapes=[pltpu.VMEM((length, HD), bf16)],
        compiler_params=pltpu.CompilerParams(vmem_limit_bytes=48 << 20),
        cost_estimate=pl.CostEstimate(flops=int(1.15e9 * (17)), bytes_accessed=1, transcendentals=0),
        name="attend_forward",
    )(projected, projected, projected, cosine, sine, *others)


def backward_kernel(block, qkv_ref, o_ref, g_ref, lse_ref, cos_ref, sin_ref, *refs):
    d_ref, sum_ref, kn_ref, vn_ref, dk_acc, dv_acc = refs
    blocks = o_ref.shape[1] // block
    kn_ref[...] = qkv_ref[1, 0].T
    vn_ref[...] = qkv_ref[2, 0].T

    def turn_back(values, cols):
        values = values.astype(bf16).astype(f32)
        return rotate(values, cos_ref[:, cols], -sin_ref[:, cols]).astype(bf16)

    for i in range(blocks):
        rows = pl.ds(i * block, block)
        q = qkv_ref[0, 0, :, rows] * jnp.asarray(HD**-0.5, bf16)
        g = g_ref[:, rows]
        lse = lse_ref[0, :, rows]
        delta = jnp.sum(g.astype(f32) * o_ref[:, rows].astype(f32), 0, keepdims=True)
        dq = None
        for j in range(i, -1, -1):
            cols = pl.ds(j * block, block)
            s = dot(kn_ref[cols, :], q, 1, 0)
            if j == i:
                s = causal(s)
            p = jnp.exp(s - lse)
            dp = dot(vn_ref[cols, :], g, 1, 0)
            ds = (p * (dp - delta)).astype(bf16)
            dv = dot(g, p.astype(bf16), 1, 1)
            dk = dot(q, ds, 1, 1)
            if j == i:
                dv_acc[:, cols] = dv
                dk_acc[:, cols] = dk
            else:
                dv_acc[:, cols] += dv
                dk_acc[:, cols] += dk
            part = dot(qkv_ref[1, 0, :, cols], ds, 1, 0)
            dq = part if dq is None else dq + part
        d_ref[0, 0, :, rows] = turn_back(dq * (HD**-0.5), rows)
    d_ref[1, 0] = turn_back(dk_acc[...], pl.ds(0, o_ref.shape[1]))
    d_ref[2, 0] = dv_acc[...].astype(bf16)
    for part in range(3):
        total = jnp.sum(d_ref[part, 0].astype(f32), 1, keepdims=True)
        sum_ref[part, 0] = jnp.broadcast_to(total, sum_ref.shape[2:])


def attend_backward(qkv, attn, d_attn, lse, cosine, sine, heads):
    length = qkv.shape[-1]
    block = length // 4
    one = pl.BlockSpec((HD, length), lambda h: (h, 0))
    three = pl.BlockSpec((3, 1, HD, length), lambda h: (0, h, 0, 0))
    table = pl.BlockSpec((ROT // 2, length), lambda h: (0, 0))
    return pl.pallas_call(
        functools.partial(backward_kernel, block),
        grid=(heads,),
        in_specs=[three, one, one, pl.BlockSpec((1, 1, length), lambda h: (h, 0, 0)), table, table],
        out_specs=[three, pl.BlockSpec((3, 1, HD, 128), lambda h: (0, h, 0, 0))],
        out_shape=[
            jax.ShapeDtypeStruct((3, heads, HD, length), bf16),
            jax.ShapeDtypeStruct((3, heads, HD, 128), f32),
        ],
        scratch_shapes=[pltpu.VMEM((length, HD), bf16)] * 2 + [pltpu.VMEM((HD, length), f32)] * 2,
        compiler_params=pltpu.CompilerParams(vmem_limit_bytes=48 << 20),
        cost_estimate=pl.CostEstimate(flops=int(1.15e9 * (28)), bytes_accessed=1, transcendentals=0),
        name="attend_backward",
    )(qkv, attn, d_attn, lse, cosine, sine)


def back_kernel(turned, core_ref, a_ref, wa_ref, b_ref, wb_ref, *refs):
    send_ref, keep_ref = refs[turned : turned + 2]
    side = 1 if turned else 0
    value = dot(a_ref[...], wa_ref[...], 0, side) + dot(b_ref[...], wb_ref[...], 0, side)
    if turned:
        hat_ref, sums_ref = refs[0], refs[3]

        @pl.when(pl.program_id(0) == 0)
        def _():
            sums_ref[...] = jnp.zeros_like(sums_ref)

        sums_ref[0:1] += jnp.sum(value * hat_ref[...].astype(f32), 0, keepdims=True)
        sums_ref[1:2] += jnp.sum(value, 0, keepdims=True)
    value = value.astype(bf16)
    rows = send_ref.shape[1]
    for core in range(2):

        @pl.when(core_ref[0] == core)
        def _():
            keep_ref[0] = value[core * rows : (core + 1) * rows]
            send_ref[0] = value[(1 - core) * rows : (2 - core) * rows]


def back_product(a, wa, b, wb, groups, hat=None):
    turned = hat is not None
    length, width = a.shape[1], wb.shape[0 if turned else 1]
    places = groups // 2
    block = length // places

    def left(value):
        return pl.BlockSpec((value.shape[0], block), lambda i, core: (0, i))

    def right(value):
        depth = value.shape[0]
        return pl.BlockSpec((width, depth) if turned else (depth, width), lambda i, core: (0, 0))

    half = jax.ShapeDtypeStruct((places, block // 2, width), bf16)
    core = (lax.axis_index("seq") % 2).astype(jnp.int32).reshape(1)
    hats = [hat] if turned else []
    return pl.pallas_call(
        functools.partial(back_kernel, turned),
        grid_spec=pltpu.PrefetchScalarGridSpec(
            num_scalar_prefetch=1,
            grid=(places,),
            in_specs=[left(a), right(a), left(b), right(b)]
            + [pl.BlockSpec((block, width), lambda i, core: (i, 0))] * len(hats),
            out_specs=[pl.BlockSpec((1, block // 2, width), lambda i, core: (i, 0, 0))] * 2
            + [pl.BlockSpec((8, width), lambda i, core: (0, 0))] * len(hats),
        ),
        out_shape=[half, half] + [jax.ShapeDtypeStruct((8, width), f32)] * len(hats),
        compiler_params=pltpu.CompilerParams(vmem_limit_bytes=56 << 20),
        cost_estimate=pl.CostEstimate(flops=int(1.15e9 * (27 if hats else 17)), bytes_accessed=1, transcendentals=0),
        name="back_product",
    )(core, a, wa, b, wb, *hats)


def normalise(values):
    average = jnp.mean(values, -1, keepdims=True)
    centred = values - average
    variance = jnp.mean(centred * centred, -1, keepdims=True)
    inverse = lax.rsqrt(variance + EPSILON)
    return centred * inverse, inverse


def gelu_tanh(values):
    scale, cubic = 0.7978845608028654, 0.044715
    curve = jnp.tanh(scale * (values + cubic * values * values * values))
    slope = 0.5 * (1.0 + curve) + 0.5 * values * (1.0 - curve * curve) * scale * (1.0 + 3.0 * cubic * values * values)
    return 0.5 * values * (1.0 + curve), slope


def rotate(parts, cosine, sine):
    half = ROT // 2
    first, second = parts[..., :half, :], parts[..., half:ROT, :]
    return jnp.concatenate(
        [first * cosine - second * sine, second * cosine + first * sine, parts[..., ROT:, :]], -2
    )


def swap(value, axes, size, bit):
    return lax.ppermute(value, axes, [(i, i ^ bit) for i in range(size)])


def gather_small(values, axis):
    index, count = lax.axis_index(axis), lax.axis_size(axis)
    block, bit = values[None], 1
    while bit < count:
        other = swap(block, axis, count, bit)
        high = (index & bit) > 0
        block = jnp.concatenate([jnp.where(high, other, block), jnp.where(high, block, other)], 0)
        bit *= 2
    return block


def scatter_small(values, size):
    index = lax.axis_index(BOTH)
    block = values
    bit = size // 2
    while bit:
        high = (index & bit) > 0
        low_half, high_half = block[:bit], block[bit:]
        other = swap(jnp.where(high, low_half, high_half), BOTH, size, bit)
        block = jnp.where(high, high_half, low_half) + other
        bit //= 2
    return block[0]


def gate(value, *others):
    anywhere = pl.BlockSpec(memory_space=pl.ANY)
    return pl.pallas_call(
        lambda *refs: None,
        in_specs=[anywhere] * (1 + len(others)),
        out_specs=anywhere,
        out_shape=jax.ShapeDtypeStruct(value.shape, value.dtype),
        input_output_aliases={0: 0},
        name="gate",
    )(value, *others)


def gather_pieces(own, wait=None):
    core = lax.axis_index("seq") % 2
    by_x = swap(own, "seq", 8, 2)
    by_y = swap(own, "seq", 8, 4)
    if wait:
        by_x = gate(by_x, *wait)
    relay = jnp.where(core == 0, by_y, by_x)
    diagonal = lax.ppermute(relay, "seq", [(i, i ^ (4 if i % 2 else 2)) for i in range(8)])
    mine = [own, by_x, by_y, diagonal]
    return [piece for one in mine for piece in (one, swap(one, "seq", 8, 1))]


def pieces_kernel(normed, order_ref, *refs):
    pieces = refs[:8]
    held = refs[-1]
    at = pl.program_id(0)
    for which, piece in enumerate(pieces):

        @pl.when(at == which)
        def _():
            held[...] = piece[...]

    if normed:
        gain_ref, shift_ref = refs[8:10]
        o_ref, hat_ref = refs[10:12]
        for at in range(0, held.shape[0], 32):
            rows = pl.ds(at, 32)
            value = normalise(held[rows, :].astype(f32))[0]
            hat_ref[rows, :] = value.astype(bf16)
            o_ref[rows, :] = (value * gain_ref[...] + shift_ref[...]).astype(bf16)


def put_in_order(pieces, *vectors, after=None):
    index = lax.axis_index("seq")
    order = jnp.stack([index ^ (2 * (which // 2)) ^ (which % 2) for which in range(8)]).astype(jnp.int32)
    rows, width = pieces[0].shape
    vectors = [vector.reshape(1, width) for vector in vectors]
    after = [] if after is None else [after]
    outs = 2 if vectors else 1
    return pl.pallas_call(
        functools.partial(pieces_kernel, bool(vectors)),
        grid_spec=pltpu.PrefetchScalarGridSpec(
            num_scalar_prefetch=1,
            grid=(8,),
            in_specs=[pl.BlockSpec((rows, width), lambda i, order: (0, 0))] * 8
            + [pl.BlockSpec((1, width), lambda i, order: (0, 0))] * len(vectors)
            + [pl.BlockSpec(memory_space=pl.ANY)] * len(after),
            out_specs=[pl.BlockSpec((rows, width), lambda i, order: (order[i], 0))] * outs,
            scratch_shapes=[pltpu.VMEM((rows, width), bf16)] * (len(vectors) > 0),
        ),
        out_shape=[jax.ShapeDtypeStruct((8 * rows, width), bf16)] * outs,
        compiler_params=pltpu.CompilerParams(vmem_limit_bytes=40 << 20),
        cost_estimate=pl.CostEstimate(flops=int(1.15e9 * (10)), bytes_accessed=1, transcendentals=0),
        name="put_in_order",
    )(order, *pieces, *vectors, *after)


def take(values, index, axis):
    return lax.dynamic_index_in_dim(values, index, axis, keepdims=False)


def sum_core(send, keep):
    return keep.astype(f32) + swap(send, "seq", 8, 1).astype(f32)


def sum_sends(cells):
    index = lax.axis_index("seq")
    x, y = (index // 2) % 2, index // 4
    half = cells.shape[2] // 2
    cells = cells.reshape(2, 2, *cells.shape[1:])
    left, right = cells[..., :half], cells[..., half:]
    sends = take(left, 1 - x, 1).astype(bf16), take(right, 1 - y, 0).astype(bf16)
    return sends, (take(left, x, 1), take(right, y, 0))


def sum_start(sends, stays):
    got_left, got_right = swap(sends[0], "seq", 8, 2), swap(sends[1], "seq", 8, 4)
    return stays[0] + got_left.astype(f32), stays[1] + got_right.astype(f32)


def sum_end(left, right):
    index = lax.axis_index("seq")
    x, y = (index // 2) % 2, index // 4
    got_left = swap(take(left, 1 - y, 0).astype(bf16), "seq", 8, 4)
    got_right = swap(take(right, 1 - x, 0).astype(bf16), "seq", 8, 2)
    left = take(left, y, 0) + got_left.astype(f32)
    right = take(right, x, 0) + got_right.astype(f32)
    return jnp.concatenate([left, right], -1)


def spread_kernel(blocks, groups, width, w_ref, o_ref):
    step = max(1, 128 // width)
    for group in range(groups):
        for at in range(0, blocks, step):
            parts = [w_ref[:, pl.ds(((at + k) * groups + group) * width, width)] for k in range(step)]
            o_ref[group, :, pl.ds(at * width, step * width)] = parts[0] if step == 1 else jnp.concatenate(parts, 1)


def collect_kernel(blocks, groups, width, g_ref, o_ref):
    step = max(1, 128 // width)
    for at in range(blocks):
        for group in range(0, groups, step):
            parts = [g_ref[group + k, :, pl.ds(at * width, width)].astype(f32) for k in range(step)]
            where = pl.ds((at * groups + group) * width, step * width)
            o_ref[:, where] = parts[0] if step == 1 else jnp.concatenate(parts, 1)


def local_call(kernel, shape, dtype, *args):
    return pl.pallas_call(
        kernel,
        out_shape=jax.ShapeDtypeStruct(shape, dtype),
        compiler_params=pltpu.CompilerParams(vmem_limit_bytes=32 << 20),
        name="regroup",
    )(*args)


def by_group(weight, blocks, groups):
    rows, width = weight.shape[0], weight.shape[1] // (blocks * groups)
    kernel = functools.partial(spread_kernel, blocks, groups, width)
    out = local_call(kernel, (groups, rows, blocks * width), bf16, weight)
    return out.reshape(groups * rows, blocks * width)


def trade(values):
    return lax.all_to_all(values, "seq", split_axis=0, concat_axis=0, tiled=True)


def to_rows(grads, groups, blocks):
    rows, width = grads.shape[0] // groups, grads.shape[1] // blocks
    got = grads.reshape(groups, rows, blocks * width)
    kernel = functools.partial(collect_kernel, blocks, groups, width)
    return local_call(kernel, (rows, blocks * groups * width), f32, got)


def local(
    block_input,
    ln_gain,
    norm_layer_bias,
    query_key_value_weight,
    query_key_value_bias,
    attention_output_weight,
    attention_output_bias,
    first_feed_weight,
    first_feed_bias,
    second_feed_weight,
    second_feed_bias,
    cotangent,
):
    shards, groups = lax.axis_size("fsdp"), lax.axis_size("seq")
    size = shards * groups
    me = lax.axis_index("seq")
    _, piece, width = block_input.shape
    length = piece * groups
    heads = H // groups
    rows = query_key_value_weight.shape[0]
    hidden_rows = second_feed_weight.shape[0]
    hidden = shards * hidden_rows
    out_rows = attention_output_weight.shape[0]
    whole_heads = out_rows == HD and heads == shards

    x_own, g_own = block_input[0], cotangent[0]
    vectors = (
        ln_gain,
        norm_layer_bias,
        query_key_value_bias,
        attention_output_bias,
        first_feed_bias,
        second_feed_bias,
    )
    small = gather_small(jnp.concatenate(vectors), "fsdp")
    small = gather_small(small, "seq").astype(f32)
    pieces, at = [], 0
    for vector in vectors:
        part = small[:, :, at : at + vector.shape[0]]
        pieces.append(part.transpose(1, 0, 2).reshape(-1))
        at += vector.shape[0]
    gain, shift, bqkv, bout, bfc1, bfc2 = pieces
    bqkv = take(bqkv.reshape(3, heads, groups, HD), me, 2).reshape(-1)
    bfc1 = take(bfc1.reshape(shards, groups, hidden_rows), me, 1).reshape(-1)
    inner = 3 * heads * HD
    wfc2 = lax.all_gather(second_feed_weight, "fsdp", axis=0, tiled=True)
    wfc1 = trade(by_group(first_feed_weight, shards, groups))
    wfc1 = lax.all_gather(gate(wfc1, wfc2), "fsdp", axis=0, tiled=True)
    first = trade(by_group(query_key_value_weight, 3 * heads, groups))
    if whole_heads:
        first = jnp.concatenate([first, attention_output_weight.reshape(groups * rows, -1)], 1)
    first = lax.all_gather(gate(first, wfc1), "fsdp", axis=0, tiled=True)
    if groups == 8:
        x_pieces = gather_pieces(x_own)
        normed_all, hat_all = put_in_order(x_pieces, gain, shift)
        (g_all,) = put_in_order(gather_pieces(gate(g_own, normed_all)))
    else:
        x_all = lax.all_gather(x_own, "seq", axis=0, tiled=True)
        hat_all = normalise(x_all.astype(f32))[0]
        normed_all = (hat_all * gain + shift).astype(bf16)
        g_all = lax.all_gather(g_own, "seq", axis=0, tiled=True)

    up_pre = dot(wfc1, normed_all, 0, 1) + bfc1[:, None]
    up, slope = gelu_tanh(up_pre)
    up = up.astype(bf16)
    term_wfc2 = dot(up, g_all, 1, 0).astype(bf16)
    d_pre = (dot(wfc2, g_all, 1, 1) * slope).astype(bf16)
    term_wfc1 = dot(normed_all, d_pre, 0, 1).astype(bf16)
    folds = width // hidden
    term_wfc1 = jnp.split(term_wfc1.reshape(shards, -1, hidden), folds, 1)
    both = jnp.concatenate([term_wfc2.reshape(shards, -1, width), jnp.concatenate(term_wfc1, 2)], 1)
    both = lax.psum_scatter(both.reshape(-1, width), "fsdp", scatter_dimension=0, tiled=True)
    grad_wfc2 = both[:hidden_rows]
    grad_wfc1 = jnp.concatenate(jnp.split(both[hidden_rows:], folds, 1), 0)

    weights_a = first
    wqkv = first[:, :inner]
    if whole_heads:
        wout = first[:, inner:].reshape(heads * HD, width)
    else:
        wout = lax.all_gather(attention_output_weight, BOTH, axis=0, tiled=True)
        wout = take(wout.reshape(heads, groups, HD, width), me, 1).reshape(heads * HD, width)
    freqs = 10000.0 ** (-2.0 * jnp.arange(ROT // 2).astype(f32) / ROT)
    angles = freqs[:, None] * jnp.arange(length).astype(f32)[None, :]
    cosine, sine = jnp.cos(angles), jnp.sin(angles)
    projected = dot(wqkv, normed_all, 0, 1) + bqkv[:, None]
    attn, lse, qkv = attend_forward(projected, cosine, sine, heads)
    d_attn = dot(wout, g_all, 1, 1).astype(bf16)
    d_proj, sum_proj = attend_backward(qkv, attn, d_attn, lse, cosine, sine, heads)
    d_proj, sum_proj = d_proj.reshape(inner, length), sum_proj[..., 0].reshape(inner)
    term_a = dot(normed_all, d_proj, 0, 1).astype(bf16)
    term_wout = dot(attn, g_all, 1, 0).astype(bf16)
    if whole_heads:
        term_a = jnp.concatenate([term_a, term_wout.reshape(width, -1)], 1)
    else:
        mask = (jnp.arange(groups) == me).astype(bf16)
        spread = term_wout.reshape(heads, 1, HD, width) * mask[None, :, None, None]
        spread = spread.reshape(H * HD, width)
        grad_wout = lax.psum_scatter(spread, BOTH, scatter_dimension=0, tiled=True).astype(f32)
    first = lax.psum_scatter(gate(term_a, both), "fsdp", scatter_dimension=0, tiled=True)

    traded = trade(grad_wfc1)
    if groups == 8:
        mixed = back_product(attn, wout, up, wfc2, groups)
        *d_normed, sums = back_product(d_proj, weights_a, d_pre, wfc1, groups, hat_all)
        mixed = sum_end(*sum_start(*sum_sends(sum_core(mixed[0], gate(mixed[1], traded)))))
        d_normed = sum_end(*sum_start(*sum_sends(sum_core(*d_normed))))
    else:
        mixed = dot(attn, wout, 0, 0) + dot(up, wfc2, 0, 0)
        d_normed = dot(d_proj, wqkv, 0, 1) + dot(d_pre, wfc1, 0, 1)
        sums = jnp.stack([jnp.sum(d_normed * hat_all, 0), jnp.sum(d_normed, 0)])
        d_normed, mixed = (
            lax.psum_scatter(v.astype(bf16), "seq", scatter_dimension=0, tiled=True).astype(f32)
            for v in (d_normed, mixed)
        )
    rows_wfc1 = to_rows(traded, groups, shards)
    grad_wfc2 = grad_wfc2.astype(f32)

    here = (jnp.arange(groups) == me).astype(f32)
    term_bqkv = sum_proj.reshape(3 * heads, 1, HD) * here[None, :, None]
    term_bqkv = term_bqkv.reshape(-1)
    term_bfc1 = (jnp.sum(d_pre.astype(f32), 1).reshape(shards, 1, hidden_rows) * here[None, :, None]).reshape(-1)
    terms = (
        sums[0],
        sums[1],
        term_bqkv[: 2 * H * HD],
        term_bqkv[2 * H * HD :],
        jnp.sum(g_own.astype(f32), 0),
        term_bfc1,
    )
    summed = jnp.concatenate([t.reshape(size, -1) for t in terms], 1)
    summed = scatter_small(summed, size)
    vector_grads, at = [], 0
    for term in terms:
        count = term.shape[0] // size
        vector_grads.append(summed[at : at + count])
        at += count
    grad_gain, grad_shift, grad_bqk, grad_bv, grad_bout, grad_bfc1 = vector_grads

    first = gate(first, mixed)
    if whole_heads:
        grad_wout = first[:, inner:].reshape(out_rows, width).astype(f32)
    grad_wqkv = to_rows(trade(first[:, :inner]), groups, 3 * heads)
    block_output = (x_own.astype(f32) + mixed + bout + bfc2).astype(bf16)
    xhat, inverse = normalise(x_own.astype(f32))
    e = d_normed * gain
    d_x = (e - jnp.mean(e, -1, keepdims=True) - xhat * jnp.mean(e * xhat, -1, keepdims=True)) * inverse
    grad_input = g_own.astype(f32) + d_x
    return (
        block_output[None],
        grad_input[None],
        grad_gain,
        grad_shift,
        grad_wqkv,
        grad_bqk,
        grad_bv,
        grad_wout,
        grad_bout,
        rows_wfc1,
        grad_bfc1,
        grad_wfc2,
        grad_bout,
    )


def solution(mesh):
    tokens, split = P("fsdp", "seq", None), P(BOTH)
    return jax.shard_map(
        local,
        mesh=mesh,
        in_specs=(tokens, *([split] * 10), tokens),
        out_specs=(tokens, tokens, *([split] * 11)),
        check_vma=False,
    )
```
